32 devices in a mesh: grp: 2 (over y), seq: 4 (over z), head: 4 (over x, core).
Axes of the slice: x: 2, y: 2, z: 4, core: 2. Of those that a mesh axis runs over, the one named last changes fastest.
Arguments:
- queries: bfloat16 [4096, 4096], P(('grp', 'seq'), 'head'), parts along dimension 0, may hold values from -6 to 6
- key_rows: bfloat16 [4096, 4096], P(('grp', 'seq'), 'head'), parts along dimension 0, may hold values from -6 to 6
- value_rows: bfloat16 [4096, 4096], P(('grp', 'seq'), 'head'), parts along dimension 0, may hold values from -6 to 6
- grad_out: bfloat16 [4096, 4096], P(('grp', 'seq'), 'head'), parts along dimension 0, may hold values from -6 to 6
- packing: int32 [6, 4], P('grp'), parts along dimension 0, may hold values from 0 to 16, as said below
Outputs:
- attended: bfloat16 [4096, 4096], P(('grp', 'seq'), 'head'), parts along dimension 0
- grad_queries: bfloat16 [4096, 4096], P(('grp', 'seq'), 'head'), parts along dimension 0
- grad_keys: bfloat16 [4096, 4096], P(('grp', 'seq'), 'head'), parts along dimension 0
- grad_values: bfloat16 [4096, 4096], P(('grp', 'seq'), 'head'), parts along dimension 0
The draws below stay inside these ranges and needn't reach their ends.
There are 2 independent parts, one for each index of `grp`. The reference program is written for one: setup_inputs(seed, part) draws one part's arguments, and reference() takes and returns one part's arrays. A program takes and returns all parts, laid end to end along the dimension named above; each array names one. Nothing has to cross between parts.
Inputs may be any that keep to these rules, and one draw needn't show every extreme that they name: `packing`: row r is the r-th segment along the sequence, in blocks of 128 tokens: row 0 starts at 0, each row starts where the previous one ends, the last ends at 16, every segment has one block or more. Rows 3p, 3p+1, 3p+2 form one pair: all carry the same pair id, the ids of the 1 pairs are 0 to 0 in some order; row 3p has role 0 (prompt), rows 3p+1 and 3p+2 have roles 1 (chosen) and 2 (rejected) in either order.
All inputs are finite; a program needn't handle non-finite values.
Results may differ from the reference program's by a relative error of at most 0.0053.
Values sent between devices are 32-bit elements; how exact they have to be, the bound alone decides.
No kernel may reach another device: no remote copies, remote signals or barrier semaphores. Data moves between devices by JAX's collectives and lax.ppermute only.
A program may use at most 128 MiB of HBM per device.

```python
import jax
import jax.numpy as jnp
from jax import lax

HEADS = 32
DH = 128
BLK = 128
GROUP = 512
TOKENS = 2048
NBLK = 16
PAIRS = 1
SEGS = 3


def draw_packing(key, part):
    key = jax.random.fold_in(key, 11)
    key_len, key_flip, key_ids = jax.random.split(key, 3)
    weights = jax.random.randint(key_len, (SEGS,), 1, 9)
    cum_weights = jnp.cumsum(weights)
    total_weight = cum_weights[-1]
    extra = NBLK - SEGS
    bounds = extra * cum_weights // total_weight
    previous = jnp.concatenate([jnp.zeros((1,), jnp.int32), bounds[:-1].astype(jnp.int32)])
    lengths = 1 + bounds.astype(jnp.int32) - previous
    seg_ends = jnp.cumsum(lengths).astype(jnp.int32)
    seg_starts = seg_ends - lengths
    flips = jax.random.randint(key_flip, (PAIRS,), 0, 2).astype(jnp.int32)
    roles = jnp.stack([jnp.zeros((PAIRS,), jnp.int32), 1 + flips, 2 - flips], axis=1).reshape(SEGS)
    pair_ids = jnp.repeat(jax.random.permutation(key_ids, PAIRS).astype(jnp.int32), 3)
    return jnp.stack([seg_starts, seg_ends, pair_ids, roles], axis=1).astype(jnp.int32)


def steps_of(key, extent, shards, smallest, largest):
    loudness, own = 1.0, jax.random.fold_in(key, 6)
    for dim, blocks in shards:
        heights = jnp.exp(jax.random.uniform(jax.random.fold_in(own, dim), (blocks,), jnp.float32, smallest / len(shards), largest / len(shards)))
        loudness = loudness * jnp.repeat(heights, extent[dim] // blocks).reshape([-1 if axis == dim else 1 for axis in range(len(extent))])
    return loudness


def gaussian(stream_key, extent, spread, limit, cuts=(), kind=jnp.bfloat16):
    drawn = spread * jax.random.normal(stream_key, extent, jnp.float32)
    if cuts:
        drawn = drawn * steps_of(stream_key, extent, cuts, -0.22, 0.18)
    return jnp.clip(drawn, -limit, limit).astype(kind)


def setup_inputs(seed: int = 0, part: int = 0) -> dict:
    key_of = jax.random.split(jax.random.key(seed), 6)
    own_keys = jax.random.split(jax.random.fold_in(key_of[5], part), 6)
    queries = gaussian(own_keys[0], (TOKENS, HEADS * DH), 1.0, 6.0, ((0, 4), (1, 4)))
    key_rows = gaussian(own_keys[1], (TOKENS, HEADS * DH), 1.0, 6.0, ((0, 4), (1, 4)))
    value_rows = gaussian(own_keys[2], (TOKENS, HEADS * DH), 1.0, 6.0, ((0, 4), (1, 4)))
    grad_out = gaussian(own_keys[3], (TOKENS, HEADS * DH), 1.0, 6.0, ((0, 4), (1, 4)))
    packing = draw_packing(jax.random.fold_in(jax.random.fold_in(key_of[5], part), 71), part)
    return {"queries": queries, "key_rows": key_rows, "value_rows": value_rows, "grad_out": grad_out, "packing": packing}


highest = lax.Precision.HIGHEST

def block_info(packing, first_block, block_count):
    seg_starts = packing[:, 0]
    seg_ends = packing[:, 1]
    pair_col = packing[:, 2]
    role_col = packing[:, 3]
    blocks = first_block + jnp.arange(block_count, dtype=jnp.int32)
    segment = lax.optimization_barrier(jnp.sum((seg_starts[None, :] <= blocks[:, None]).astype(jnp.int32), axis=1)) - 1
    seg_ranks = jnp.arange(seg_starts.shape[0], dtype=jnp.int32)
    select = segment[:, None] == seg_ranks[None, :]
    block_role = lax.optimization_barrier(jnp.sum(jnp.where(select, role_col[None, :], 0), axis=1))
    block_pair = lax.optimization_barrier(jnp.sum(jnp.where(select, pair_col[None, :], 0), axis=1))
    opening = lax.optimization_barrier(jnp.sum(jnp.where(select, seg_starts[None, :], 0), axis=1))
    prompt_sel = (segment // 3 * 3)[:, None] == seg_ranks[None, :]
    prompt_len = lax.optimization_barrier(jnp.sum(jnp.where(prompt_sel, (seg_ends - seg_starts)[None, :], 0), axis=1))
    position = (blocks - opening)[:, None] * BLK + jnp.arange(BLK, dtype=jnp.int32)[None, :]
    visible = position + 1 + jnp.where(block_role != 0, prompt_len * BLK, 0)[:, None]
    tok_scale = lax.rsqrt((visible * DH).astype(jnp.float32))
    return (segment, block_role, block_pair, tok_scale)

def reference(queries, key_rows, value_rows, grad_out, packing):
    block_total = TOKENS // BLK
    group_total = TOKENS // GROUP
    segment, block_role, block_pair, tok_scale = block_info(packing, 0, block_total)
    dpo_sign = jnp.where(block_role == 2, -1.0, 1.0).astype(jnp.float32)
    group_of = jnp.arange(block_total, dtype=jnp.int32) // (GROUP // BLK)
    same_seg = segment[:, None] == segment[None, :]
    feeds = (block_role[:, None] != 0) & (block_role[None, :] == 0) & (block_pair[:, None] == block_pair[None, :])
    link = (same_seg & (group_of[None, :] < group_of[:, None]) | feeds).astype(jnp.float32)
    tok_seg = jnp.repeat(segment, BLK).reshape(group_total, GROUP)
    places = jnp.arange(GROUP, dtype=jnp.int32)
    causal = (tok_seg[:, :, None] == tok_seg[:, None, :]) & (places[None, :, None] >= places[None, None, :])
    weight = (dpo_sign[:, None] * tok_scale)[:, :, None]
    scale_b = tok_scale[:, :, None]

    def one_head(head):

        def cut(array):
            return lax.dynamic_slice_in_dim(array, head * DH, DH, 1).astype(jnp.float32)
        qf = cut(queries)
        kf = cut(key_rows)
        vf = cut(value_rows)
        gin = cut(grad_out)
        qb = qf.reshape(block_total, BLK, DH)
        kb = kf.reshape(block_total, BLK, DH)
        vb = vf.reshape(block_total, BLK, DH)
        block_kv = jnp.einsum('bsd,bse->bde', kb, vb, precision=highest)
        state = jnp.einsum('bj,jde->bde', link, block_kv, precision=highest)
        qc = qf.reshape(group_total, GROUP, DH)
        kc = kf.reshape(group_total, GROUP, DH)
        vc = vf.reshape(group_total, GROUP, DH)
        scores = jnp.einsum('csd,ctd->cst', qc, kc, precision=highest)
        attn_weights = jnp.where(causal, scores, 0.0).astype(jnp.bfloat16).astype(jnp.float32)
        inside = jnp.einsum('cst,ctd->csd', attn_weights, vc, precision=highest).reshape(block_total, BLK, DH)
        outside = jnp.einsum('bsd,bde->bse', qb, state, precision=highest)
        attended = (scale_b * (inside + outside)).astype(jnp.bfloat16)
        g_rows = (weight * gin.reshape(block_total, BLK, DH)).astype(jnp.bfloat16).astype(jnp.float32)
        gc = g_rows.reshape(group_total, GROUP, DH)
        back_raw = jnp.einsum('csd,ctd->cst', gc, vc, precision=highest)
        back_weights = jnp.where(causal, back_raw, 0.0).astype(jnp.bfloat16).astype(jnp.float32)
        block_qg = jnp.einsum('bsd,bse->bde', qb, g_rows, precision=highest)
        back_state = jnp.einsum('bj,bde->jde', link, block_qg, precision=highest)
        grad_q = jnp.einsum('cst,ctd->csd', back_weights, kc, precision=highest).reshape(block_total, BLK, DH)
        grad_q = grad_q + jnp.einsum('bse,bde->bsd', g_rows, state, precision=highest)
        grad_k = jnp.einsum('cst,csd->ctd', back_weights, qc, precision=highest).reshape(block_total, BLK, DH)
        grad_k = grad_k + jnp.einsum('bse,bde->bsd', vb, back_state, precision=highest)
        grad_v = jnp.einsum('cst,csd->ctd', attn_weights, gc, precision=highest).reshape(block_total, BLK, DH)
        grad_v = grad_v + jnp.einsum('bsd,bde->bse', kb, back_state, precision=highest)
        return (attended.reshape(TOKENS, DH), grad_q.astype(jnp.bfloat16).reshape(TOKENS, DH), grad_k.astype(jnp.bfloat16).reshape(TOKENS, DH), grad_v.astype(jnp.bfloat16).reshape(TOKENS, DH))
    results = lax.map(one_head, jnp.arange(HEADS, dtype=jnp.int32))

    def arrange(stacked):
        return jnp.transpose(stacked, (1, 0, 2)).reshape(TOKENS, HEADS * DH)
    return (arrange(results[0]), arrange(results[1]), arrange(results[2]), arrange(results[3]))
```

```python
import functools

import jax
import jax.numpy as jnp
from jax import lax
from jax.experimental import pallas as pl
from jax.experimental.pallas import tpu as pltpu
from jax.sharding import PartitionSpec as P

DH = 128
BLK = 128
GROUP = 512
NB = GROUP // BLK
CHUNKS = 2
F32 = jnp.float32
BF16 = jnp.bfloat16


def flag(condition):
    return jnp.where(condition, 1, 0).astype(jnp.int32)


def either(*flags):
    out = flags[0]
    for f in flags[1:]:
        out = jnp.maximum(out, f)
    return out


def pick(index, choices):
    out = jnp.int32(0) + choices[-1]
    for n in range(len(choices) - 2, -1, -1):
        out = jnp.where(index == n, choices[n], out)
    return out


def pick_rows(index, rows):
    return [pick(index, [row[c] for row in rows]) for c in range(len(rows[0]))]


def edges(pack, blocks):
    one, two = pack[1, 0], pack[2, 0]

    def seg(b):
        return flag(b >= one) + flag(b >= two)

    first = [seg(blocks * i) for i in range(4)]
    last = [seg(blocks * i + blocks - 1) for i in range(4)]
    return seg, first, last


def message_one(pack, d, blocks):
    _, f, l = edges(pack, blocks)
    every = either(flag(l[2] == 0), flag(l[2] == 1) * flag(l[1] == 0))
    at_p, from_p = flag(l[0] == 0), flag(f[2] == 0)
    return pick_rows(
        d,
        [
            [1, 1, flag(f[2] == 1), flag(f[2] == 2)],
            [at_p, at_p, 0, 1 - at_p],
            [from_p, 0, from_p * flag(f[3] == 1), from_p * flag(f[3] == 2) + 1 - from_p],
            [0, every, either(every, flag(l[2] == 1)), either(every, flag(l[2] == 2))],
        ],
    )


def message_two(pack, d, blocks):
    _, f, l = edges(pack, blocks)
    return pick_rows(
        d,
        [
            [flag(l[0] == 0), 1, 1, 0, 0],
            [1, 1, 1, flag(f[2] == 1), flag(f[2] == 2)],
            [
                1 - flag(l[1] == 1) * flag(l[2] == 2),
                0,
                flag(l[1] == 0),
                flag(l[1] <= 1),
                flag(l[1] != 1),
            ],
            [flag(f[2] != 0), 0, 0, 0, 1],
        ],
    )


def message_three(pack, d, blocks):
    _, f, l = edges(pack, blocks)
    from_p, at_p, first_p = flag(f[2] == 0), flag(l[1] == 0), flag(f[1] == 0)
    return pick_rows(
        d,
        [
            [first_p, 1, 0, 1 - first_p, 0],
            [
                1 - flag(l[0] == 1) * flag(l[1] == 2),
                0,
                flag(l[0] == 0),
                flag(l[0] <= 1),
                flag(l[0] != 1),
            ],
            [
                either(from_p, flag(f[2] == f[3])),
                1,
                from_p,
                (1 - from_p) * flag(f[3] == 1),
                (1 - from_p) * flag(f[3] == 2),
            ],
            [1 - at_p, 0, 0, at_p, 0],
        ],
    )


def state_table(pack, d, blocks):
    _, f, l = edges(pack, blocks)
    apart = flag(f[2] == 1) * flag(l[1] != 0)
    from_p = flag(f[2] == 0)
    crossing = (1 - from_p) * flag(f[3] == 1)
    forward = [
        pick_rows(d, [[0, 0, 0], [1, 0, 0], [0, 1, 0], [0, 0, 1]]),
        pick_rows(
            d,
            [
                [0, 0, 0],
                [1, 0, flag(f[1] == 1) * flag(f[2] == 2)],
                [0, 1, 0],
                [from_p * flag(f[3] == 1), 0, 1],
            ],
        ),
        pick_rows(
            d,
            [
                [0, 0, 0],
                [1, 0, 0],
                [0, 1 - apart, apart],
                [
                    from_p * flag(f[3] == 2),
                    either(crossing, (1 - from_p) * flag(f[2] != f[3])),
                    1 - crossing,
                ],
            ],
        ),
    ]
    backward = [
        pick_rows(
            d,
            [
                [
                    flag(l[0] == 1),
                    either(flag(l[0] == 1), flag(l[0] == 0) * flag(l[1] == 1)),
                    1,
                ],
                [0, 1, flag(l[1] == 1)],
                [1, 0, 0],
                [0, 0, 0],
            ],
        ),
        pick_rows(
            d,
            [
                [0, 0, flag(l[0] == 1)],
                [0, flag(l[1] == 1), 0],
                [flag(l[2] == 1) * flag(l[1] != 0), 0, flag(l[2] == 1) * flag(l[1] == 0)],
                [0, 0, 0],
            ],
        ),
        pick_rows(
            d,
            [
                [0, 0, flag(l[0] == 2)],
                [0, flag(l[1] == 2), 0],
                [flag(l[2] == 2), 0, 0],
                [0, 0, 0],
            ],
        ),
    ]
    return forward, backward


def block_rows(value_of, like):
    return jnp.concatenate([jnp.full((BLK, like), value_of(b), F32) for b in range(NB)], axis=0)


def fill_scale(pack, d, blocks, scale_ref, sign_ref):
    seg, _, _ = edges(pack, blocks)
    prompt = pack[0, 1] - pack[0, 0]
    for b in range(NB):
        block = d * blocks + b
        s = seg(block)
        start = pick(s, [pack[0, 0], pack[1, 0], pack[2, 0]])
        role = pick(s, [pack[0, 3], pack[1, 3], pack[2, 3]])
        base = (block - start) * BLK + 1 + jnp.where(role != 0, prompt * BLK, 0)
        seen = base + lax.broadcasted_iota(jnp.int32, (BLK, DH), 0)
        scale = lax.rsqrt((seen * DH).astype(F32))
        rows = pl.ds(b * BLK, BLK)
        if scale_ref is not None:
            scale_ref[rows, :] = scale
        if sign_ref is not None:
            sign_ref[rows, :] = jnp.where(role == 2, -1.0, 1.0) * scale


def weighted(grad, sign_ref):
    return (grad.astype(F32) * sign_ref[...]).astype(BF16)


def contract_rows(a, b):
    return lax.dot_general(a, b, (((0,), (0,)), ((), ())), preferred_element_type=F32)


def contract_cols(a, b):
    return lax.dot_general(a, b, (((1,), (1,)), ((), ())), preferred_element_type=F32)


def plain(a, b):
    return lax.dot_general(a, b, (((1,), (0,)), ((), ())), preferred_element_type=F32)


def row_mask(pack, d, blocks, coefs):
    seg, _, _ = edges(pack, blocks)
    return block_rows(lambda b: pick(seg(d * blocks + b), coefs).astype(F32), DH).astype(BF16)


def sums_kernel(blocks, per_step, messages, pack, place, q_ref, k_ref, v_ref, g_ref, *refs):
    outs, sign_ref = refs[:-1], refs[-1]
    d = place[0]
    step = pl.program_id(0)

    @pl.when(step == 0)
    def _():
        fill_scale(pack, d, blocks, None, sign_ref)

    tables = [m(pack, d, blocks)[-4:] for m in messages]
    masks = [row_mask(pack, d, blocks, t[1:]) for t in tables]
    per_chunk = pl.num_programs(0) // CHUNKS

    def emit(index, head, value):
        for c in range(CHUNKS):

            @pl.when(step // per_chunk == c)
            def _():
                outs[index * CHUNKS + c][head] = value

    for head in range(per_step):
        cols = pl.ds(head * DH, DH)
        for index, (table, mask) in enumerate(zip(tables, masks)):

            @pl.when(table[0] == 1)
            def _():
                emit(index, head, contract_rows(k_ref[:, cols] * mask, v_ref[:, cols]))

            @pl.when(table[0] == 0)
            def _():
                grads = weighted(g_ref[:, cols], sign_ref)
                emit(index, head, contract_rows(q_ref[:, cols] * mask, grads))


def local_sums(messages, blocks, pack, place, q, k, v, g):
    heads = q.shape[1] // DH
    per_step = 2 if heads % (2 * CHUNKS) == 0 else 1
    steps = heads // per_step
    per_chunk = steps // CHUNKS

    def needed(kind):
        def index(i, pack_ref, place_ref):
            use = jnp.int32(0)
            for m in messages:
                use = either(use, flag(m(pack_ref, place_ref[0], blocks)[-4] == kind))
            return (0, i * use)

        return index

    def chunk(c):
        return lambda i, *_: (jnp.clip(i - c * per_chunk, 0, per_chunk - 1), 0, 0)

    rows = q.shape[0]
    tokens = (rows, per_step * DH)
    out = jax.ShapeDtypeStruct((heads // CHUNKS, DH, DH), F32)
    return pl.pallas_call(
        functools.partial(sums_kernel, blocks, per_step, messages),
        out_shape=[out] * (CHUNKS * len(messages)),
        grid_spec=pltpu.PrefetchScalarGridSpec(
            num_scalar_prefetch=2,
            grid=(steps,),
            in_specs=[
                pl.BlockSpec(tokens, needed(0)),
                pl.BlockSpec(tokens, needed(1)),
                pl.BlockSpec(tokens, needed(1)),
                pl.BlockSpec(tokens, needed(0)),
            ],
            out_specs=[
                pl.BlockSpec((per_step, DH, DH), chunk(c)) for _ in messages for c in range(CHUNKS)
            ],
            scratch_shapes=[pltpu.VMEM((rows, DH), F32)],
        ),
        compiler_params=pltpu.CompilerParams(vmem_limit_bytes=16 * 2**20),
        cost_estimate=pl.CostEstimate(
            flops=2 * rows * DH * DH * heads * len(messages),
            bytes_accessed=4 * rows * heads * DH,
            transcendentals=0,
        ),
        name="local_sums",
    )(pack, place, q, k, v, g)


def join_kernel(blocks, message, pack, place, got_ref, own_ref, out_ref):
    keep = message(pack, place[0], blocks)[0] == 1

    @pl.when(keep)
    def _():
        out_ref[...] = got_ref[...] + own_ref[...]

    @pl.when(jnp.logical_not(keep))
    def _():
        out_ref[...] = own_ref[...]


def join(message, blocks, pack, place, got, own):
    heads = got.shape[0]
    return pl.pallas_call(
        functools.partial(join_kernel, blocks, message),
        out_shape=jax.ShapeDtypeStruct(got.shape, F32),
        grid_spec=pltpu.PrefetchScalarGridSpec(
            num_scalar_prefetch=2,
            grid=(1,),
            in_specs=[pl.BlockSpec((heads, DH, DH), lambda i, *_: (0, 0, 0))] * 2,
            out_specs=pl.BlockSpec((heads, DH, DH), lambda i, *_: (0, 0, 0)),
        ),
        compiler_params=pltpu.CompilerParams(vmem_limit_bytes=8 * 2**20),
        cost_estimate=pl.CostEstimate(
            flops=got.size, bytes_accessed=12 * got.size, transcendentals=0
        ),
        name="join",
    )(pack, place, got, own)


def inside_kernel(blocks, pack, place, q_ref, k_ref, v_ref, g_ref, o1, o2, o3, o4, mask_ref, sign_ref):
    d = place[0]
    half = GROUP // 2

    @pl.when(pl.program_id(0) == 0)
    def _():
        fill_scale(pack, d, blocks, None, sign_ref)
        seg, _, _ = edges(pack, blocks)
        tri = lax.broadcasted_iota(jnp.int32, (BLK, BLK), 0) >= lax.broadcasted_iota(
            jnp.int32, (BLK, BLK), 1
        )
        for t in range(NB):
            for s in range(NB):
                seg_t, seg_s = seg(d * blocks + t), seg(d * blocks + s)
                ok = either(flag(seg_t == seg_s), flag(seg_s == 0)).astype(F32)
                if s > t:
                    tile = jnp.zeros((BLK, BLK), F32)
                elif s == t:
                    tile = jnp.where(tri, 1.0, 0.0)
                else:
                    tile = jnp.full((BLK, BLK), ok, F32)
                mask_ref[pl.ds(t * BLK, BLK), pl.ds(s * BLK, BLK)] = tile.astype(BF16)

    q, k, v = q_ref[...], k_ref[...], v_ref[...]
    g = weighted(g_ref[...], sign_ref)
    lo, hi = slice(0, half), slice(half, GROUP)

    def masked(a, b, rows, cols):
        return contract_cols(a[rows], b[cols]).astype(BF16) * mask_ref[rows, cols]

    s_lo = masked(q, k, lo, lo)
    s_hi = masked(q, k, hi, slice(0, GROUP))
    o1[lo, :] = plain(s_lo, v[lo])
    o1[hi, :] = plain(s_hi, v)
    gv = contract_rows(s_hi, g[hi])
    o4[lo, :] = gv[lo] + contract_rows(s_lo, g[lo])
    o4[hi, :] = gv[hi]
    b_lo = masked(g, v, lo, lo)
    b_hi = masked(g, v, hi, slice(0, GROUP))
    o2[lo, :] = plain(b_lo, k[lo])
    o2[hi, :] = plain(b_hi, k)
    gk = contract_rows(b_hi, q[hi])
    o3[lo, :] = gk[lo] + contract_rows(b_lo, q[lo])
    o3[hi, :] = gk[hi]


def inside_products(blocks, pack, place, q, k, v, g):
    rows, cols = q.shape
    heads = cols // DH
    spec = pl.BlockSpec((rows, DH), lambda i, *_: (0, i))
    return pl.pallas_call(
        functools.partial(inside_kernel, blocks),
        out_shape=[jax.ShapeDtypeStruct((rows, cols), F32)] * 4,
        grid_spec=pltpu.PrefetchScalarGridSpec(
            num_scalar_prefetch=2,
            grid=(heads,),
            in_specs=[spec] * 4,
            out_specs=[spec] * 4,
            scratch_shapes=[pltpu.VMEM((rows, rows), BF16), pltpu.VMEM((rows, DH), F32)],
        ),
        compiler_params=pltpu.CompilerParams(vmem_limit_bytes=24 * 2**20),
        cost_estimate=pl.CostEstimate(
            flops=9 * rows * rows * DH * heads,
            bytes_accessed=24 * rows * cols,
            transcendentals=0,
        ),
        name="inside_products",
    )(pack, place, q, k, v, g)


def final_kernel(blocks, first, pack, place, *refs):
    q_ref, k_ref, v_ref, g_ref, i1, i2, i3, i4, r1, r2, r3 = refs[:11]
    o1, o2, o3, o4, scale_ref, sign_ref, st_ref, bk_ref = refs[-8:]
    d = place[0]

    @pl.when(pl.program_id(0) == 0)
    def _():
        fill_scale(pack, d, blocks, scale_ref, sign_ref)

    seg, _, _ = edges(pack, blocks)
    forward, backward = state_table(pack, d, blocks)
    got = [r1[0], r2[0], r3[0]]
    for x in range(3):
        for table, out in ((forward, st_ref), (backward, bk_ref)):
            total = None
            for weight, part in zip(table[x], got):
                term = weight.astype(F32) * part
                total = term if total is None else total + term
            out[x] = total.astype(BF16)
    for b in range(NB):
        rows = pl.ds(b * BLK, BLK)
        s = seg(d * blocks + b)
        st, bk = st_ref[s], bk_ref[s]
        q, k, v = q_ref[rows, :], k_ref[rows, :], v_ref[rows, :]
        g = (g_ref[rows, :].astype(F32) * sign_ref[rows, :]).astype(BF16)
        o1[rows, :] = (scale_ref[rows, :] * (i1[rows, :] + plain(q, st))).astype(BF16)
        o2[rows, :] = (i2[rows, :] + contract_cols(g, st)).astype(BF16)
        o3[rows, :] = (i3[rows, :] + contract_cols(v, bk)).astype(BF16)
        o4[rows, :] = (i4[rows, :] + plain(k, bk)).astype(BF16)


def final_products(blocks, chunk, pack, place, tokens, inside, got, before):
    rows, cols = tokens[0].shape
    heads = cols // DH // CHUNKS
    first = chunk * heads
    spec = pl.BlockSpec((rows, DH), lambda i, *_: (0, first + i))
    state = pl.BlockSpec((1, DH, DH), lambda i, *_: (i, 0, 0))
    operands = [*tokens, *inside, *got]
    specs = [spec] * 8 + [state] * 3
    aliases = {}
    if before is not None:
        aliases = {2 + len(operands) + n: n for n in range(4)}
        operands += list(before)
        specs += [pl.BlockSpec(memory_space=pl.ANY)] * 4
    return pl.pallas_call(
        functools.partial(final_kernel, blocks, first),
        out_shape=[jax.ShapeDtypeStruct((rows, cols), BF16)] * 4,
        grid_spec=pltpu.PrefetchScalarGridSpec(
            num_scalar_prefetch=2,
            grid=(heads,),
            in_specs=specs,
            out_specs=[spec] * 4,
            scratch_shapes=[
                pltpu.VMEM((rows, DH), F32),
                pltpu.VMEM((rows, DH), F32),
                pltpu.VMEM((3, DH, DH), BF16),
                pltpu.VMEM((3, DH, DH), BF16),
            ],
        ),
        input_output_aliases=aliases,
        compiler_params=pltpu.CompilerParams(vmem_limit_bytes=16 * 2**20),
        cost_estimate=pl.CostEstimate(
            flops=8 * rows * DH * DH * heads,
            bytes_accessed=32 * rows * DH * heads,
            transcendentals=0,
        ),
        name="final_products",
    )(pack, place, *operands)


def exchange_body(queries, key_rows, value_rows, grad_out, packing):
    blocks = queries.shape[0] // BLK
    place = lax.axis_index("seq").astype(jnp.int32).reshape(1)
    tokens = (queries, key_rows, value_rows, grad_out)
    near = [(i, i ^ 1) for i in range(4)]
    across = [(i, 3 - i) for i in range(4)]

    def send(values, pairs):
        return [lax.ppermute(value, "seq", pairs) for value in values]

    sent = local_sums((message_one,), blocks, packing, place, *tokens)
    one = send(sent, near)
    own = local_sums((message_two, message_three), blocks, packing, place, *tokens)
    own_two, own_three = own[:CHUNKS], own[CHUNKS:]
    inside = inside_products(blocks, packing, place, *tokens)
    two = send(
        [join(message_two, blocks, packing, place, a, b) for a, b in zip(one, own_two)], across
    )
    three = send(
        [join(message_three, blocks, packing, place, a, b) for a, b in zip(two, own_three)], near
    )
    out = None
    for c in range(CHUNKS):
        out = final_products(
            blocks, c, packing, place, tokens, inside, (one[c], two[c], three[c]), out
        )
    return tuple(out)


highest = lax.Precision.HIGHEST


def carried_in(value, axis, combine, identity, reverse):
    length, index = (lax.axis_size(axis), lax.axis_index(axis))
    everything = jax.tree.map(lambda part: lax.all_gather(part, axis), value)
    start = jax.tree.map(
        lambda part, zero: jnp.broadcast_to(jnp.asarray(zero, part.dtype), part.shape),
        value,
        identity,
    )

    def turn(k, before):
        at = length - 1 - k if reverse else k
        reached = at > index if reverse else at < index
        new = combine(before, jax.tree.map(lambda part: part[at], everything))
        return jax.tree.map(lambda a, b: jnp.where(reached, a, b), new, before)

    return lax.fori_loop(0, length, turn, start)


def block_info(packing, first_block, block_count):
    seg_starts = packing[:, 0]
    seg_ends = packing[:, 1]
    pair_col = packing[:, 2]
    role_col = packing[:, 3]
    blocks = first_block + jnp.arange(block_count, dtype=jnp.int32)
    segment = jnp.sum((seg_starts[None, :] <= blocks[:, None]).astype(jnp.int32), axis=1) - 1
    seg_ranks = jnp.arange(seg_starts.shape[0], dtype=jnp.int32)
    select = segment[:, None] == seg_ranks[None, :]
    block_role = jnp.sum(jnp.where(select, role_col[None, :], 0), axis=1)
    block_pair = jnp.sum(jnp.where(select, pair_col[None, :], 0), axis=1)
    opening = jnp.sum(jnp.where(select, seg_starts[None, :], 0), axis=1)
    prompt_sel = (segment // 3 * 3)[:, None] == seg_ranks[None, :]
    prompt_len = jnp.sum(jnp.where(prompt_sel, (seg_ends - seg_starts)[None, :], 0), axis=1)
    position = (blocks - opening)[:, None] * BLK + jnp.arange(BLK, dtype=jnp.int32)[None, :]
    visible = position + 1 + jnp.where(block_role != 0, prompt_len * BLK, 0)[:, None]
    tok_scale = lax.rsqrt((visible * DH).astype(jnp.float32))
    return (segment, block_role, block_pair, tok_scale)


def link_combine(before, behind):
    back_a, open_a, state_a = before
    back_b, open_b, state_b = behind
    empty_b = open_b < 0.0
    joins = (back_b == open_b) & (open_a == back_b) | empty_b
    state = state_b + jnp.where(joins, state_a, jnp.zeros_like(state_a))
    back_id = jnp.where(open_a < 0.0, back_b, back_a)
    open_id = jnp.where(empty_b, open_a, open_b)
    return (back_id, open_id, state)


def pick_state(carry_open, carry_state, block_ids, allowed):
    chosen = (carry_open == block_ids.astype(jnp.float32)) & allowed
    return jnp.where(chosen[:, None, None, None], carry_state[None], 0.0)


def masked_sum(flags, states):
    return jnp.einsum("j,jhde->hde", flags.astype(jnp.float32), states, precision=highest)


def split_state(state):
    upper = state.astype(jnp.bfloat16)
    upper_wide = lax.optimization_barrier(upper).astype(jnp.float32)
    lower = (state - upper_wide).astype(jnp.bfloat16)
    return (upper, lower)


def state_product(form, token_rows, parts):
    first = jnp.einsum(form, token_rows, parts[0], preferred_element_type=jnp.float32)
    return first + jnp.einsum(form, token_rows, parts[1], preferred_element_type=jnp.float32)


def body(queries, key_rows, value_rows, grad_out, packing):
    block_count = queries.shape[0] // BLK
    local_heads = queries.shape[1] // DH
    group_count = queries.shape[0] // GROUP
    final_index = block_count - 1
    first_block = lax.axis_index("seq") * block_count
    segment, block_role, block_pair, tok_scale = block_info(packing, first_block, block_count)
    dpo_sign = jnp.where(block_role == 2, -1.0, 1.0).astype(jnp.float32)
    q_blocks = queries.reshape(block_count, BLK, local_heads, DH)
    k_blocks = key_rows.reshape(block_count, BLK, local_heads, DH)
    v_blocks = value_rows.reshape(block_count, BLK, local_heads, DH)
    weight = (dpo_sign[:, None] * tok_scale)[:, :, None, None]
    g_blocks = (
        weight * grad_out.reshape(block_count, BLK, local_heads, DH).astype(jnp.float32)
    ).astype(jnp.bfloat16)
    block_kv = jnp.einsum("bshd,bshe->bhde", k_blocks, v_blocks, preferred_element_type=jnp.float32)
    block_qg = jnp.einsum("bshd,bshe->bhde", q_blocks, g_blocks, preferred_element_type=jnp.float32)
    group_of = jnp.arange(block_count, dtype=jnp.int32) // (GROUP // BLK)
    same_seg = segment[:, None] == segment[None, :]
    link = same_seg & (group_of[None, :] < group_of[:, None])
    seg_first = segment[0].astype(jnp.float32)
    seg_last = segment[final_index].astype(jnp.float32)
    neutral = jnp.full((), -1.0, jnp.float32)
    zero_state = jnp.zeros((local_heads, DH, DH), jnp.float32)
    is_prompt = block_role == 0
    is_reply = block_role != 0
    pair_count = packing.shape[0] // 3
    pair_hot = (block_pair[:, None] == jnp.arange(pair_count, dtype=jnp.int32)[None, :]).astype(
        jnp.float32
    )
    fwd_seg = masked_sum(segment == segment[final_index], block_kv)
    carried = carried_in(
        (seg_first, seg_last, fwd_seg), "seq", link_combine, (neutral, neutral, zero_state), False
    )
    prompt_part = jnp.einsum(
        "jp,jhde->phde",
        pair_hot * is_prompt[:, None].astype(jnp.float32),
        block_kv,
        precision=highest,
    )
    prompt_all = lax.psum(prompt_part, "seq")
    outside_in = pick_state(carried[1], carried[2], segment, is_reply | is_prompt)
    outside_in = outside_in + jnp.einsum(
        "bp,phde->bhde",
        pair_hot * is_reply[:, None].astype(jnp.float32),
        prompt_all,
        precision=highest,
    )
    rev_seg = masked_sum(segment == segment[0], block_qg)
    returned = carried_in(
        (seg_last, seg_first, rev_seg), "seq", link_combine, (neutral, neutral, zero_state), True
    )
    reply_part = jnp.einsum(
        "jp,jhde->phde",
        pair_hot * is_reply[:, None].astype(jnp.float32),
        block_qg,
        precision=highest,
    )
    reply_all = lax.psum(reply_part, "seq")
    outside_back = pick_state(returned[1], returned[2], segment, is_reply | is_prompt)
    outside_back = outside_back + jnp.einsum(
        "bp,phde->bhde",
        pair_hot * is_prompt[:, None].astype(jnp.float32),
        reply_all,
        precision=highest,
    )
    link_f = link.astype(jnp.float32)
    state = jnp.einsum("bj,jhde->bhde", link_f, block_kv, precision=highest) + outside_in
    back_state = jnp.einsum("bj,bhde->jhde", link_f, block_qg, precision=highest) + outside_back
    state_parts = split_state(state)
    back_parts = split_state(back_state)
    tok_seg = jnp.repeat(segment, BLK).reshape(group_count, GROUP)
    places = jnp.arange(GROUP, dtype=jnp.int32)
    causal = (tok_seg[:, :, None] == tok_seg[:, None, :]) & (
        places[None, :, None] >= places[None, None, :]
    )
    q_groups = queries.reshape(group_count, GROUP, local_heads, DH)
    k_groups = key_rows.reshape(group_count, GROUP, local_heads, DH)
    v_groups = value_rows.reshape(group_count, GROUP, local_heads, DH)
    g_groups = g_blocks.reshape(group_count, GROUP, local_heads, DH)
    scores = jnp.einsum("cshd,cthd->chst", q_groups, k_groups, preferred_element_type=jnp.float32)
    attn_weights = jnp.where(causal[:, None], scores, 0.0).astype(jnp.bfloat16)
    inside = jnp.einsum(
        "chst,cthd->cshd", attn_weights, v_groups, preferred_element_type=jnp.float32
    )
    inside = inside.reshape(block_count, BLK, local_heads, DH)
    outside = state_product("bshd,bhde->bshe", q_blocks, state_parts)
    attended = (tok_scale[:, :, None, None] * (inside + outside)).astype(jnp.bfloat16)
    back_raw = jnp.einsum("cshd,cthd->chst", g_groups, v_groups, preferred_element_type=jnp.float32)
    back_weights = jnp.where(causal[:, None], back_raw, 0.0).astype(jnp.bfloat16)
    grad_q = jnp.einsum(
        "chst,cthd->cshd", back_weights, k_groups, preferred_element_type=jnp.float32
    )
    grad_q = grad_q.reshape(block_count, BLK, local_heads, DH)
    grad_q = grad_q + state_product("bshe,bhde->bshd", g_blocks, state_parts)
    grad_k = jnp.einsum(
        "chst,cshd->cthd", back_weights, q_groups, preferred_element_type=jnp.float32
    )
    grad_k = grad_k.reshape(block_count, BLK, local_heads, DH)
    grad_k = grad_k + state_product("bshe,bhde->bshd", v_blocks, back_parts)
    grad_v = jnp.einsum(
        "chst,cshd->cthd", attn_weights, g_groups, preferred_element_type=jnp.float32
    )
    grad_v = grad_v.reshape(block_count, BLK, local_heads, DH)
    grad_v = grad_v + state_product("bshd,bhde->bshe", k_blocks, back_parts)
    rows = queries.shape[0]
    columns = queries.shape[1]
    return (
        attended.reshape(rows, columns),
        grad_q.astype(jnp.bfloat16).reshape(rows, columns),
        grad_k.astype(jnp.bfloat16).reshape(rows, columns),
        grad_v.astype(jnp.bfloat16).reshape(rows, columns),
    )


def solution(mesh):
    placed = (
        P(("grp", "seq"), "head"),
        P(("grp", "seq"), "head"),
        P(("grp", "seq"), "head"),
        P(("grp", "seq"), "head"),
        P("grp", None),
    )
    pairs_of = lambda packing: packing.shape[0] // mesh.shape["grp"] // 3

    def program(queries, key_rows, value_rows, grad_out, packing):
        small = mesh.shape["seq"] == 4 and pairs_of(packing) == 1
        rows = queries.shape[0] // mesh.shape["grp"] // mesh.shape["seq"]
        fits = rows == GROUP and queries.shape[1] // mesh.shape["head"] % (CHUNKS * DH) == 0
        return placed_call(exchange_body if small and fits else body)(
            queries, key_rows, value_rows, grad_out, packing
        )

    placed_call = lambda one: jax.shard_map(
        one,
        mesh=mesh,
        in_specs=placed,
        out_specs=(
            P(("grp", "seq"), "head"),
            P(("grp", "seq"), "head"),
            P(("grp", "seq"), "head"),
            P(("grp", "seq"), "head"),
        ),
        check_vma=False,
    )
    return program
```

```python
import functools

import jax
import jax.numpy as jnp
from jax import lax
from jax.experimental import pallas as pl
from jax.experimental.pallas import tpu as pltpu
from jax.sharding import PartitionSpec as P

DH = 128
BLK = 128
GROUP = 512
NB = GROUP // BLK
SIZES = (4, 4)
ORDER = (("two", 0), ("two", 1), ("in", 0), ("three", 0), ("three", 1), ("end", 0), ("end", 1))
HELD = jnp.bfloat16
F32 = jnp.float32
BF16 = jnp.bfloat16
MIB = 2**20
SUMS_LIMIT = 60 * MIB
JOIN_LIMIT = 4 * MIB
IN_LIMIT = 16 * MIB
END_LIMIT = 16 * MIB


def flag(condition):
    return jnp.where(condition, 1, 0).astype(jnp.int32)


def either(*flags):
    out = flags[0]
    for f in flags[1:]:
        out = jnp.maximum(out, f)
    return out


def pick(index, choices):
    out = jnp.int32(0) + choices[-1]
    for n in range(len(choices) - 2, -1, -1):
        out = jnp.where(index == n, choices[n], out)
    return out


def pick_rows(index, rows):
    return [pick(index, [row[c] for row in rows]) for c in range(len(rows[0]))]


def edges(pack, blocks):
    one, two = pack[1, 0], pack[2, 0]

    def seg(b):
        return flag(b >= one) + flag(b >= two)

    first = [seg(blocks * i) for i in range(4)]
    last = [seg(blocks * i + blocks - 1) for i in range(4)]
    return seg, first, last


def message_one(pack, d, blocks):
    _, f, l = edges(pack, blocks)
    every = either(flag(l[2] == 0), flag(l[2] == 1) * flag(l[1] == 0))
    at_p, from_p = flag(l[0] == 0), flag(f[2] == 0)
    return pick_rows(
        d,
        [
            [1, 1, flag(f[2] == 1), flag(f[2] == 2)],
            [at_p, at_p, 0, 1 - at_p],
            [from_p, 0, from_p * flag(f[3] == 1), from_p * flag(f[3] == 2) + 1 - from_p],
            [0, every, either(every, flag(l[2] == 1)), either(every, flag(l[2] == 2))],
        ],
    )


def message_two(pack, d, blocks):
    _, f, l = edges(pack, blocks)
    return pick_rows(
        d,
        [
            [flag(l[0] == 0), 1, 1, 0, 0],
            [1, 1, 1, flag(f[2] == 1), flag(f[2] == 2)],
            [
                1 - flag(l[1] == 1) * flag(l[2] == 2),
                0,
                flag(l[1] == 0),
                flag(l[1] <= 1),
                flag(l[1] != 1),
            ],
            [flag(f[2] != 0), 0, 0, 0, 1],
        ],
    )


def message_three(pack, d, blocks):
    _, f, l = edges(pack, blocks)
    from_p, at_p, first_p = flag(f[2] == 0), flag(l[1] == 0), flag(f[1] == 0)
    return pick_rows(
        d,
        [
            [first_p, 1, 0, 1 - first_p, 0],
            [
                1 - flag(l[0] == 1) * flag(l[1] == 2),
                0,
                flag(l[0] == 0),
                flag(l[0] <= 1),
                flag(l[0] != 1),
            ],
            [
                either(from_p, flag(f[2] == f[3])),
                1,
                from_p,
                (1 - from_p) * flag(f[3] == 1),
                (1 - from_p) * flag(f[3] == 2),
            ],
            [1 - at_p, 0, 0, at_p, 0],
        ],
    )


def state_table(pack, d, blocks):
    _, f, l = edges(pack, blocks)
    apart = flag(f[2] == 1) * flag(l[1] != 0)
    from_p = flag(f[2] == 0)
    crossing = (1 - from_p) * flag(f[3] == 1)
    forward = [
        pick_rows(d, [[0, 0, 0], [1, 0, 0], [0, 1, 0], [0, 0, 1]]),
        pick_rows(
            d,
            [
                [0, 0, 0],
                [1, 0, flag(f[1] == 1) * flag(f[2] == 2)],
                [0, 1, 0],
                [from_p * flag(f[3] == 1), 0, 1],
            ],
        ),
        pick_rows(
            d,
            [
                [0, 0, 0],
                [1, 0, 0],
                [0, 1 - apart, apart],
                [
                    from_p * flag(f[3] == 2),
                    either(crossing, (1 - from_p) * flag(f[2] != f[3])),
                    1 - crossing,
                ],
            ],
        ),
    ]
    backward = [
        pick_rows(
            d,
            [
                [
                    flag(l[0] == 1),
                    either(flag(l[0] == 1), flag(l[0] == 0) * flag(l[1] == 1)),
                    1,
                ],
                [0, 1, flag(l[1] == 1)],
                [1, 0, 0],
                [0, 0, 0],
            ],
        ),
        pick_rows(
            d,
            [
                [0, 0, flag(l[0] == 1)],
                [0, flag(l[1] == 1), 0],
                [flag(l[2] == 1) * flag(l[1] != 0), 0, flag(l[2] == 1) * flag(l[1] == 0)],
                [0, 0, 0],
            ],
        ),
        pick_rows(
            d,
            [
                [0, 0, flag(l[0] == 2)],
                [0, flag(l[1] == 2), 0],
                [flag(l[2] == 2), 0, 0],
                [0, 0, 0],
            ],
        ),
    ]
    return forward, backward


SMEM = pl.BlockSpec(memory_space=pltpu.SMEM)
ANY = pl.BlockSpec(memory_space=pl.ANY)
VMEM = pl.BlockSpec(memory_space=pltpu.VMEM)


def fill_scale(pack, d, scale_ref, sign_ref):
    seg, _, _ = edges(pack, NB)
    prompt = pack[0, 1] - pack[0, 0]
    for b in range(NB):
        block = d * NB + b
        s = seg(block)
        start = pick(s, [pack[0, 0], pack[1, 0], pack[2, 0]])
        role = pick(s, [pack[0, 3], pack[1, 3], pack[2, 3]])
        base = (block - start) * BLK + 1 + jnp.where(role != 0, prompt * BLK, 0)
        seen = base + lax.broadcasted_iota(jnp.int32, (BLK, DH), 0)
        scale = lax.rsqrt((seen * DH).astype(F32))
        rows = pl.ds(b * BLK, BLK)
        if scale_ref is not None:
            scale_ref[rows, :] = scale
        sign_ref[rows, :] = jnp.where(role == 2, -1.0, 1.0) * scale


def weighted(rows, weight):
    return (rows.astype(F32) * weight).astype(BF16)


def contract_rows(a, b):
    return lax.dot_general(a, b, (((0,), (0,)), ((), ())), preferred_element_type=F32)


def contract_cols(a, b):
    return lax.dot_general(a, b, (((1,), (1,)), ((), ())), preferred_element_type=F32)


def plain(a, b):
    return lax.dot_general(a, b, (((1,), (0,)), ((), ())), preferred_element_type=F32)


def sums_kernel(messages, sizes, pack, place, q_hbm, k_hbm, v_hbm, g_hbm, after, *refs):
    many, heads = len(messages), sum(sizes)
    outs = refs[: many * len(sizes)]
    left, right, weight_ref, sign_ref, sems = refs[many * len(sizes) :]
    d = place[0]
    seg, _, _ = edges(pack, NB)
    tables = [m(pack, d, NB)[-4:] for m in messages]

    def copies(m, source_left, source_right):
        out = []
        for h in range(heads):
            cols = pl.ds(h * DH, DH)
            out.append(
                [
                    pltpu.make_async_copy(src.at[:, cols], dst.at[m, :, cols], sems.at[m, n, h])
                    for n, (src, dst) in enumerate(((source_left, left), (source_right, right)))
                ]
            )
        return out

    for m in range(many):
        for kind, sources in ((1, (k_hbm, v_hbm)), (0, (q_hbm, g_hbm))):

            @pl.when(tables[m][0] == kind)
            def _():
                for both in copies(m, *sources):
                    for copy in both:
                        copy.start()

    fill_scale(pack, d, None, sign_ref)
    for m in range(many):
        forward = tables[m][0] == 1
        for b in range(NB):
            rows = pl.ds(b * BLK, BLK)
            takes = pick(seg(d * NB + b), tables[m][1:]).astype(F32)
            weight_ref[m, rows, :] = jnp.where(forward, 1.0, sign_ref[rows, :]) * takes
    waits = [copies(m, k_hbm, v_hbm) for m in range(many)]
    for m in range(many):
        h = 0
        for c, size in enumerate(sizes):
            for inner in range(size):
                for copy in waits[m][h]:
                    copy.wait()
                cols = pl.ds(h * DH, DH)
                rows = weighted(right[m, :, cols], weight_ref[m])
                outs[m * len(sizes) + c][inner] = contract_rows(left[m, :, cols], rows)
                h += 1


def local_sums(messages, sizes, scalars, tokens, after):
    rows, heads, many = tokens[0].shape[0], sum(sizes), len(messages)
    out = pl.pallas_call(
        functools.partial(sums_kernel, messages, sizes),
        out_shape=[
            jax.ShapeDtypeStruct((size, DH, DH), F32) for _ in messages for size in sizes
        ],
        in_specs=[SMEM, SMEM] + [ANY] * 5,
        out_specs=[VMEM] * (many * len(sizes)),
        scratch_shapes=[
            pltpu.VMEM((many, rows, heads * DH), BF16),
            pltpu.VMEM((many, rows, heads * DH), BF16),
            pltpu.VMEM((many, rows, DH), F32),
            pltpu.VMEM((rows, DH), F32),
            pltpu.SemaphoreType.DMA((many, 2, heads)),
        ],
        compiler_params=pltpu.CompilerParams(vmem_limit_bytes=SUMS_LIMIT),
        cost_estimate=pl.CostEstimate(
            flops=2 * rows * DH * DH * heads * many,
            bytes_accessed=8 * rows * heads * DH * many,
            transcendentals=0,
        ),
        name="local_sums",
    )(*scalars, *tokens, after)
    return [out[m * len(sizes) : (m + 1) * len(sizes)] for m in range(many)]


def join_kernel(message, pack, place, got_ref, own_ref, after, out_ref):
    keep = message(pack, place[0], NB)[0] == 1

    @pl.when(keep)
    def _():
        out_ref[...] = got_ref[...] + own_ref[...]

    @pl.when(jnp.logical_not(keep))
    def _():
        out_ref[...] = own_ref[...]


def join(message, scalars, got, own, after):
    return pl.pallas_call(
        functools.partial(join_kernel, message),
        out_shape=jax.ShapeDtypeStruct(got.shape, F32),
        in_specs=[SMEM, SMEM, VMEM, VMEM, ANY],
        out_specs=VMEM,
        compiler_params=pltpu.CompilerParams(vmem_limit_bytes=JOIN_LIMIT),
        cost_estimate=pl.CostEstimate(
            flops=got.size, bytes_accessed=12 * got.size, transcendentals=0
        ),
        name="join",
    )(*scalars, got, own, after)


def inside_kernel(per, pack, place, q_ref, k_ref, v_ref, g_ref, after, o1, o2, o3, o4, mask_ref, sign_ref):
    d = place[0]
    half = GROUP // 2

    @pl.when(pl.program_id(0) == 0)
    def _():
        fill_scale(pack, d, None, sign_ref)
        seg, _, _ = edges(pack, NB)
        segs = [seg(d * NB + b) for b in range(NB)]
        tri = lax.broadcasted_iota(jnp.int32, (BLK, BLK), 0) >= lax.broadcasted_iota(
            jnp.int32, (BLK, BLK), 1
        )
        for t in range(NB):
            for s in range(NB):
                if s > t:
                    tile = jnp.zeros((BLK, BLK), F32)
                elif s == t:
                    tile = jnp.where(tri, 1.0, 0.0)
                else:
                    sees = either(flag(segs[t] == segs[s]), flag(segs[s] == 0))
                    tile = jnp.full((BLK, BLK), sees.astype(F32))
                mask_ref[pl.ds(t * BLK, BLK), pl.ds(s * BLK, BLK)] = tile.astype(BF16)

    lo, hi, whole = slice(0, half), slice(half, GROUP), slice(0, GROUP)
    for h in range(per):
        cols = slice(h * DH, (h + 1) * DH)
        q, k, v = q_ref[:, cols], k_ref[:, cols], v_ref[:, cols]
        g = weighted(g_ref[:, cols], sign_ref[...])

        def masked(a, b, rows, keys):
            return contract_cols(a[rows], b[keys]).astype(BF16) * mask_ref[rows, keys]

        def put(ref, rows, value):
            ref[rows, cols] = value.astype(ref.dtype)

        s_lo = masked(q, k, lo, lo)
        s_hi = masked(q, k, hi, whole)
        put(o1, lo, plain(s_lo, v[lo]))
        put(o1, hi, plain(s_hi, v))
        gv = contract_rows(s_hi, g[hi])
        put(o4, lo, gv[lo] + contract_rows(s_lo, g[lo]))
        put(o4, hi, gv[hi])
        b_lo = masked(g, v, lo, lo)
        b_hi = masked(g, v, hi, whole)
        put(o2, lo, plain(b_lo, k[lo]))
        put(o2, hi, plain(b_hi, k))
        gk = contract_rows(b_hi, q[hi])
        put(o3, lo, gk[lo] + contract_rows(b_lo, q[lo]))
        put(o3, hi, gk[hi])


def inside_products(scalars, tokens, after):
    rows, heads = tokens[0].shape[0], tokens[0].shape[1] // DH
    per = 2 if heads % 2 == 0 else 1
    spec = pl.BlockSpec((rows, per * DH), lambda i: (0, i))
    return pl.pallas_call(
        functools.partial(inside_kernel, per),
        out_shape=[jax.ShapeDtypeStruct((rows, heads * DH), HELD)] * 4,
        grid=(heads // per,),
        in_specs=[SMEM, SMEM] + [spec] * 4 + [ANY],
        out_specs=[spec] * 4,
        scratch_shapes=[pltpu.VMEM((rows, rows), BF16), pltpu.VMEM((rows, DH), F32)],
        compiler_params=pltpu.CompilerParams(vmem_limit_bytes=IN_LIMIT),
        cost_estimate=pl.CostEstimate(
            flops=9 * rows * rows * DH * heads,
            bytes_accessed=16 * rows * heads * DH,
            transcendentals=0,
        ),
        name="inside_products",
    )(*scalars, *tokens, after)


def final_kernel(per, pack, place, *refs):
    q_ref, k_ref, v_ref, g_ref, i1, i2, i3, i4, r1, r2, r3 = refs[:11]
    o1, o2, o3, o4, scale_ref, sign_ref, st_ref, bk_ref = refs[-8:]
    d = place[0]

    @pl.when(pl.program_id(0) == 0)
    def _():
        fill_scale(pack, d, scale_ref, sign_ref)

    seg, _, _ = edges(pack, NB)
    forward, backward = state_table(pack, d, NB)
    for h in range(per):
        cols = slice(h * DH, (h + 1) * DH)
        got = [r1[h], r2[h], r3[h]]
        for x in range(3):
            for table, out in ((forward, st_ref), (backward, bk_ref)):
                total = None
                for weight, part in zip(table[x], got):
                    term = weight.astype(F32) * part
                    total = term if total is None else total + term
                out[x] = total.astype(BF16)
        for b in range(NB):
            rows = pl.ds(b * BLK, BLK)
            s = seg(d * NB + b)
            st, bk = st_ref[s], bk_ref[s]
            q, k, v = q_ref[rows, cols], k_ref[rows, cols], v_ref[rows, cols]
            g = weighted(g_ref[rows, cols], sign_ref[rows, :])

            def put(ref, held, value, scale=None):
                total = held[rows, cols].astype(F32) + value
                ref[rows, cols] = (total if scale is None else scale * total).astype(BF16)

            put(o1, i1, plain(q, st), scale_ref[rows, :])
            put(o2, i2, contract_cols(g, st))
            put(o3, i3, contract_cols(v, bk))
            put(o4, i4, plain(k, bk))


def final_products(first, heads, scalars, tokens, inside, got, before):
    rows, cols = tokens[0].shape
    per = 2 if first % 2 == 0 and heads % 2 == 0 else 1
    spec = pl.BlockSpec((rows, per * DH), lambda i: (0, first // per + i))
    state = pl.BlockSpec((per, DH, DH), lambda i: (i, 0, 0))
    operands = [*scalars, *tokens, *inside, *got]
    specs = [SMEM, SMEM] + [spec] * 8 + [state] * 3
    aliases = {}
    if before is not None:
        aliases = {len(operands) + n: n for n in range(4)}
        operands += list(before)
        specs += [ANY] * 4
    return pl.pallas_call(
        functools.partial(final_kernel, per),
        out_shape=[jax.ShapeDtypeStruct((rows, cols), BF16)] * 4,
        grid=(heads // per,),
        in_specs=specs,
        out_specs=[spec] * 4,
        scratch_shapes=[
            pltpu.VMEM((rows, DH), F32),
            pltpu.VMEM((rows, DH), F32),
            pltpu.VMEM((3, DH, DH), BF16),
            pltpu.VMEM((3, DH, DH), BF16),
        ],
        input_output_aliases=aliases,
        compiler_params=pltpu.CompilerParams(vmem_limit_bytes=END_LIMIT),
        cost_estimate=pl.CostEstimate(
            flops=8 * rows * DH * DH * heads,
            bytes_accessed=28 * rows * DH * heads,
            transcendentals=0,
        ),
        name="final_products",
    )(*operands)


def exchange_body(queries, key_rows, value_rows, grad_out, packing):
    place = lax.axis_index("seq").astype(jnp.int32).reshape(1)
    scalars = (packing, place)
    tokens = (queries, key_rows, value_rows, grad_out)
    starts = [sum(SIZES[:c]) for c in range(len(SIZES))]
    near = [(i, i ^ 1) for i in range(4)]
    across = [(i, 3 - i) for i in range(4)]

    (early,) = local_sums((message_one,), SIZES, scalars, tokens, packing)
    one = [lax.ppermute(value, "seq", near) for value in early]
    own_two, own_three = local_sums((message_two, message_three), SIZES, scalars, tokens, early[0])
    last = own_two[0]
    two, three = [None] * len(SIZES), [None] * len(SIZES)
    out = None
    for what, c in ORDER:
        if what == "two":
            last = join(message_two, scalars, one[c], own_two[c], last)
            two[c] = lax.ppermute(last, "seq", across)
        elif what == "three":
            last = join(message_three, scalars, two[c], own_three[c], last)
            three[c] = lax.ppermute(last, "seq", near)
        elif what == "in":
            inside = inside_products(scalars, tokens, last)
            last = inside[0]
        else:
            got = (one[c], two[c], three[c])
            out = final_products(starts[c], SIZES[c], scalars, tokens, inside, got, out)
    return tuple(out)


highest = lax.Precision.HIGHEST


def carried_in(value, axis, combine, identity, reverse):
    length, index = (lax.axis_size(axis), lax.axis_index(axis))
    everything = jax.tree.map(lambda part: lax.all_gather(part, axis), value)
    start = jax.tree.map(
        lambda part, zero: jnp.broadcast_to(jnp.asarray(zero, part.dtype), part.shape),
        value,
        identity,
    )

    def turn(k, before):
        at = length - 1 - k if reverse else k
        reached = at > index if reverse else at < index
        new = combine(before, jax.tree.map(lambda part: part[at], everything))
        return jax.tree.map(lambda a, b: jnp.where(reached, a, b), new, before)

    return lax.fori_loop(0, length, turn, start)


def block_info(packing, first_block, block_count):
    seg_starts = packing[:, 0]
    seg_ends = packing[:, 1]
    pair_col = packing[:, 2]
    role_col = packing[:, 3]
    blocks = first_block + jnp.arange(block_count, dtype=jnp.int32)
    segment = jnp.sum((seg_starts[None, :] <= blocks[:, None]).astype(jnp.int32), axis=1) - 1
    seg_ranks = jnp.arange(seg_starts.shape[0], dtype=jnp.int32)
    select = segment[:, None] == seg_ranks[None, :]
    block_role = jnp.sum(jnp.where(select, role_col[None, :], 0), axis=1)
    block_pair = jnp.sum(jnp.where(select, pair_col[None, :], 0), axis=1)
    opening = jnp.sum(jnp.where(select, seg_starts[None, :], 0), axis=1)
    prompt_sel = (segment // 3 * 3)[:, None] == seg_ranks[None, :]
    prompt_len = jnp.sum(jnp.where(prompt_sel, (seg_ends - seg_starts)[None, :], 0), axis=1)
    position = (blocks - opening)[:, None] * BLK + jnp.arange(BLK, dtype=jnp.int32)[None, :]
    visible = position + 1 + jnp.where(block_role != 0, prompt_len * BLK, 0)[:, None]
    tok_scale = lax.rsqrt((visible * DH).astype(jnp.float32))
    return (segment, block_role, block_pair, tok_scale)


def link_combine(before, behind):
    back_a, open_a, state_a = before
    back_b, open_b, state_b = behind
    empty_b = open_b < 0.0
    joins = (back_b == open_b) & (open_a == back_b) | empty_b
    state = state_b + jnp.where(joins, state_a, jnp.zeros_like(state_a))
    back_id = jnp.where(open_a < 0.0, back_b, back_a)
    open_id = jnp.where(empty_b, open_a, open_b)
    return (back_id, open_id, state)


def pick_state(carry_open, carry_state, block_ids, allowed):
    chosen = (carry_open == block_ids.astype(jnp.float32)) & allowed
    return jnp.where(chosen[:, None, None, None], carry_state[None], 0.0)


def masked_sum(flags, states):
    return jnp.einsum("j,jhde->hde", flags.astype(jnp.float32), states, precision=highest)


def split_state(state):
    upper = state.astype(jnp.bfloat16)
    upper_wide = lax.optimization_barrier(upper).astype(jnp.float32)
    lower = (state - upper_wide).astype(jnp.bfloat16)
    return (upper, lower)


def state_product(form, token_rows, parts):
    first = jnp.einsum(form, token_rows, parts[0], preferred_element_type=jnp.float32)
    return first + jnp.einsum(form, token_rows, parts[1], preferred_element_type=jnp.float32)


def body(queries, key_rows, value_rows, grad_out, packing):
    block_count = queries.shape[0] // BLK
    local_heads = queries.shape[1] // DH
    group_count = queries.shape[0] // GROUP
    final_index = block_count - 1
    first_block = lax.axis_index("seq") * block_count
    segment, block_role, block_pair, tok_scale = block_info(packing, first_block, block_count)
    dpo_sign = jnp.where(block_role == 2, -1.0, 1.0).astype(jnp.float32)
    q_blocks = queries.reshape(block_count, BLK, local_heads, DH)
    k_blocks = key_rows.reshape(block_count, BLK, local_heads, DH)
    v_blocks = value_rows.reshape(block_count, BLK, local_heads, DH)
    weight = (dpo_sign[:, None] * tok_scale)[:, :, None, None]
    g_blocks = (
        weight * grad_out.reshape(block_count, BLK, local_heads, DH).astype(jnp.float32)
    ).astype(jnp.bfloat16)
    block_kv = jnp.einsum("bshd,bshe->bhde", k_blocks, v_blocks, preferred_element_type=jnp.float32)
    block_qg = jnp.einsum("bshd,bshe->bhde", q_blocks, g_blocks, preferred_element_type=jnp.float32)
    group_of = jnp.arange(block_count, dtype=jnp.int32) // (GROUP // BLK)
    same_seg = segment[:, None] == segment[None, :]
    link = same_seg & (group_of[None, :] < group_of[:, None])
    seg_first = segment[0].astype(jnp.float32)
    seg_last = segment[final_index].astype(jnp.float32)
    neutral = jnp.full((), -1.0, jnp.float32)
    zero_state = jnp.zeros((local_heads, DH, DH), jnp.float32)
    is_prompt = block_role == 0
    is_reply = block_role != 0
    pair_count = packing.shape[0] // 3
    pair_hot = (block_pair[:, None] == jnp.arange(pair_count, dtype=jnp.int32)[None, :]).astype(
        jnp.float32
    )
    fwd_seg = masked_sum(segment == segment[final_index], block_kv)
    carried = carried_in(
        (seg_first, seg_last, fwd_seg), "seq", link_combine, (neutral, neutral, zero_state), False
    )
    prompt_part = jnp.einsum(
        "jp,jhde->phde",
        pair_hot * is_prompt[:, None].astype(jnp.float32),
        block_kv,
        precision=highest,
    )
    prompt_all = lax.psum(prompt_part, "seq")
    outside_in = pick_state(carried[1], carried[2], segment, is_reply | is_prompt)
    outside_in = outside_in + jnp.einsum(
        "bp,phde->bhde",
        pair_hot * is_reply[:, None].astype(jnp.float32),
        prompt_all,
        precision=highest,
    )
    rev_seg = masked_sum(segment == segment[0], block_qg)
    returned = carried_in(
        (seg_last, seg_first, rev_seg), "seq", link_combine, (neutral, neutral, zero_state), True
    )
    reply_part = jnp.einsum(
        "jp,jhde->phde",
        pair_hot * is_reply[:, None].astype(jnp.float32),
        block_qg,
        precision=highest,
    )
    reply_all = lax.psum(reply_part, "seq")
    outside_back = pick_state(returned[1], returned[2], segment, is_reply | is_prompt)
    outside_back = outside_back + jnp.einsum(
        "bp,phde->bhde",
        pair_hot * is_prompt[:, None].astype(jnp.float32),
        reply_all,
        precision=highest,
    )
    link_f = link.astype(jnp.float32)
    state = jnp.einsum("bj,jhde->bhde", link_f, block_kv, precision=highest) + outside_in
    back_state = jnp.einsum("bj,bhde->jhde", link_f, block_qg, precision=highest) + outside_back
    state_parts = split_state(state)
    back_parts = split_state(back_state)
    tok_seg = jnp.repeat(segment, BLK).reshape(group_count, GROUP)
    places = jnp.arange(GROUP, dtype=jnp.int32)
    causal = (tok_seg[:, :, None] == tok_seg[:, None, :]) & (
        places[None, :, None] >= places[None, None, :]
    )
    q_groups = queries.reshape(group_count, GROUP, local_heads, DH)
    k_groups = key_rows.reshape(group_count, GROUP, local_heads, DH)
    v_groups = value_rows.reshape(group_count, GROUP, local_heads, DH)
    g_groups = g_blocks.reshape(group_count, GROUP, local_heads, DH)
    scores = jnp.einsum("cshd,cthd->chst", q_groups, k_groups, preferred_element_type=jnp.float32)
    attn_weights = jnp.where(causal[:, None], scores, 0.0).astype(jnp.bfloat16)
    inside = jnp.einsum(
        "chst,cthd->cshd", attn_weights, v_groups, preferred_element_type=jnp.float32
    )
    inside = inside.reshape(block_count, BLK, local_heads, DH)
    outside = state_product("bshd,bhde->bshe", q_blocks, state_parts)
    attended = (tok_scale[:, :, None, None] * (inside + outside)).astype(jnp.bfloat16)
    back_raw = jnp.einsum("cshd,cthd->chst", g_groups, v_groups, preferred_element_type=jnp.float32)
    back_weights = jnp.where(causal[:, None], back_raw, 0.0).astype(jnp.bfloat16)
    grad_q = jnp.einsum(
        "chst,cthd->cshd", back_weights, k_groups, preferred_element_type=jnp.float32
    )
    grad_q = grad_q.reshape(block_count, BLK, local_heads, DH)
    grad_q = grad_q + state_product("bshe,bhde->bshd", g_blocks, state_parts)
    grad_k = jnp.einsum(
        "chst,cshd->cthd", back_weights, q_groups, preferred_element_type=jnp.float32
    )
    grad_k = grad_k.reshape(block_count, BLK, local_heads, DH)
    grad_k = grad_k + state_product("bshe,bhde->bshd", v_blocks, back_parts)
    grad_v = jnp.einsum(
        "chst,cshd->cthd", attn_weights, g_groups, preferred_element_type=jnp.float32
    )
    grad_v = grad_v.reshape(block_count, BLK, local_heads, DH)
    grad_v = grad_v + state_product("bshd,bhde->bshe", k_blocks, back_parts)
    rows = queries.shape[0]
    columns = queries.shape[1]
    return (
        attended.reshape(rows, columns),
        grad_q.astype(jnp.bfloat16).reshape(rows, columns),
        grad_k.astype(jnp.bfloat16).reshape(rows, columns),
        grad_v.astype(jnp.bfloat16).reshape(rows, columns),
    )


def solution(mesh):
    tokens = P(("grp", "seq"), "head")

    def program(queries, key_rows, value_rows, grad_out, packing):
        rows = queries.shape[0] // mesh.shape["grp"] // mesh.shape["seq"]
        heads = queries.shape[1] // mesh.shape["head"] // DH
        pairs = packing.shape[0] // mesh.shape["grp"] // 3
        four = mesh.shape["seq"] == 4 and pairs == 1
        fits = rows == GROUP and heads == sum(SIZES)
        return jax.shard_map(
            exchange_body if four and fits else body,
            mesh=mesh,
            in_specs=(tokens,) * 4 + (P("grp", None),),
            out_specs=(tokens,) * 4,
            check_vma=False,
        )(queries, key_rows, value_rows, grad_out, packing)

    return program
```

```python
import functools

import jax
import jax.numpy as jnp
from jax import lax
from jax.experimental import pallas as pl
from jax.experimental.pallas import tpu as pltpu
from jax.sharding import PartitionSpec as P

DH = 128
BLK = 128
GROUP = 512
NB = GROUP // BLK
SIZES = (4, 4)
IN_SIZES = (4, 4)
ORDER = (
    ("one", 0),
    ("own_two", 0),
    ("early", 0),
    ("one", 1),
    ("two", 0),
    ("own_three", 0),
    ("in", 0),
    ("two", 1),
    ("in", 1),
    ("three", 0),
    ("three", 1),
    ("end", 0),
    ("end", 1),
)
MIB = 2**20
FIRST_LIMIT = 60 * MIB
SUMS_LIMIT = 12 * MIB
JOIN_LIMIT = 4 * MIB
IN_LIMIT = 16 * MIB
END_LIMIT = 16 * MIB
HELD = jnp.bfloat16
F32 = jnp.float32
BF16 = jnp.bfloat16


def flag(condition):
    return jnp.where(condition, 1, 0).astype(jnp.int32)


def either(*flags):
    out = flags[0]
    for f in flags[1:]:
        out = jnp.maximum(out, f)
    return out


def pick(index, choices):
    out = jnp.int32(0) + choices[-1]
    for n in range(len(choices) - 2, -1, -1):
        out = jnp.where(index == n, choices[n], out)
    return out


def pick_rows(index, rows):
    return [pick(index, [row[c] for row in rows]) for c in range(len(rows[0]))]


def edges(pack, blocks):
    one, two = pack[1, 0], pack[2, 0]

    def seg(b):
        return flag(b >= one) + flag(b >= two)

    first = [seg(blocks * i) for i in range(4)]
    last = [seg(blocks * i + blocks - 1) for i in range(4)]
    return seg, first, last


def message_one(pack, d, blocks):
    _, f, l = edges(pack, blocks)
    every = either(flag(l[2] == 0), flag(l[2] == 1) * flag(l[1] == 0))
    at_p, from_p = flag(l[0] == 0), flag(f[2] == 0)
    return pick_rows(
        d,
        [
            [1, 1, flag(f[2] == 1), flag(f[2] == 2)],
            [at_p, at_p, 0, 1 - at_p],
            [from_p, 0, from_p * flag(f[3] == 1), from_p * flag(f[3] == 2) + 1 - from_p],
            [0, every, either(every, flag(l[2] == 1)), either(every, flag(l[2] == 2))],
        ],
    )


def message_two(pack, d, blocks):
    _, f, l = edges(pack, blocks)
    return pick_rows(
        d,
        [
            [flag(l[0] == 0), 1, 1, 0, 0],
            [1, 1, 1, flag(f[2] == 1), flag(f[2] == 2)],
            [
                1 - flag(l[1] == 1) * flag(l[2] == 2),
                0,
                flag(l[1] == 0),
                flag(l[1] <= 1),
                flag(l[1] != 1),
            ],
            [flag(f[2] != 0), 0, 0, 0, 1],
        ],
    )


def message_three(pack, d, blocks):
    _, f, l = edges(pack, blocks)
    from_p, at_p, first_p = flag(f[2] == 0), flag(l[1] == 0), flag(f[1] == 0)
    return pick_rows(
        d,
        [
            [first_p, 1, 0, 1 - first_p, 0],
            [
                1 - flag(l[0] == 1) * flag(l[1] == 2),
                0,
                flag(l[0] == 0),
                flag(l[0] <= 1),
                flag(l[0] != 1),
            ],
            [
                either(from_p, flag(f[2] == f[3])),
                1,
                from_p,
                (1 - from_p) * flag(f[3] == 1),
                (1 - from_p) * flag(f[3] == 2),
            ],
            [1 - at_p, 0, 0, at_p, 0],
        ],
    )


def state_table(pack, d, blocks):
    _, f, l = edges(pack, blocks)
    apart = flag(f[2] == 1) * flag(l[1] != 0)
    from_p = flag(f[2] == 0)
    crossing = (1 - from_p) * flag(f[3] == 1)
    forward = [
        pick_rows(d, [[0, 0, 0], [1, 0, 0], [0, 1, 0], [0, 0, 1]]),
        pick_rows(
            d,
            [
                [0, 0, 0],
                [1, 0, flag(f[1] == 1) * flag(f[2] == 2)],
                [0, 1, 0],
                [from_p * flag(f[3] == 1), 0, 1],
            ],
        ),
        pick_rows(
            d,
            [
                [0, 0, 0],
                [1, 0, 0],
                [0, 1 - apart, apart],
                [
                    from_p * flag(f[3] == 2),
                    either(crossing, (1 - from_p) * flag(f[2] != f[3])),
                    1 - crossing,
                ],
            ],
        ),
    ]
    backward = [
        pick_rows(
            d,
            [
                [
                    flag(l[0] == 1),
                    either(flag(l[0] == 1), flag(l[0] == 0) * flag(l[1] == 1)),
                    1,
                ],
                [0, 1, flag(l[1] == 1)],
                [1, 0, 0],
                [0, 0, 0],
            ],
        ),
        pick_rows(
            d,
            [
                [0, 0, flag(l[0] == 1)],
                [0, flag(l[1] == 1), 0],
                [flag(l[2] == 1) * flag(l[1] != 0), 0, flag(l[2] == 1) * flag(l[1] == 0)],
                [0, 0, 0],
            ],
        ),
        pick_rows(
            d,
            [
                [0, 0, flag(l[0] == 2)],
                [0, flag(l[1] == 2), 0],
                [flag(l[2] == 2), 0, 0],
                [0, 0, 0],
            ],
        ),
    ]
    return forward, backward


SHORT = pl.CostEstimate(flops=1, bytes_accessed=1, transcendentals=0)
SMEM = pl.BlockSpec(memory_space=pltpu.SMEM)
ANY = pl.BlockSpec(memory_space=pl.ANY)
HBM = pl.BlockSpec(memory_space=pltpu.HBM)
VMEM = pl.BlockSpec(memory_space=pltpu.VMEM)


def fill_scale(pack, d, scale_ref, sign_ref):
    seg, _, _ = edges(pack, NB)
    prompt = pack[0, 1] - pack[0, 0]
    for b in range(NB):
        block = d * NB + b
        s = seg(block)
        start = pick(s, [pack[0, 0], pack[1, 0], pack[2, 0]])
        role = pick(s, [pack[0, 3], pack[1, 3], pack[2, 3]])
        base = (block - start) * BLK + 1 + jnp.where(role != 0, prompt * BLK, 0)
        seen = base + lax.broadcasted_iota(jnp.int32, (BLK, DH), 0)
        scale = lax.rsqrt((seen * DH).astype(F32))
        rows = pl.ds(b * BLK, BLK)
        if scale_ref is not None:
            scale_ref[rows, :] = scale
        sign_ref[rows, :] = jnp.where(role == 2, -1.0, 1.0) * scale


def weighted(rows, weight):
    return (rows.astype(F32) * weight).astype(BF16)


def contract_rows(a, b):
    return lax.dot_general(a, b, (((0,), (0,)), ((), ())), preferred_element_type=F32)


def contract_cols(a, b):
    return lax.dot_general(a, b, (((1,), (1,)), ((), ())), preferred_element_type=F32)


def plain(a, b):
    return lax.dot_general(a, b, (((1,), (0,)), ((), ())), preferred_element_type=F32)


def sums_kernel(messages, first, sizes, pack, place, q_hbm, k_hbm, v_hbm, g_hbm, after, *refs):
    many, chunks = len(messages), len(sizes)
    outs = refs[: many * chunks]
    left, right, total, weight_ref, sign_ref, in_sems, out_sems = refs[many * chunks :]
    d = place[0]
    seg, _, _ = edges(pack, NB)
    tables = [m(pack, d, NB)[-4:] for m in messages]
    starts = [sum(sizes[:c]) for c in range(chunks)]

    def copies(m, c, sources):
        there = pl.ds((first + starts[c]) * DH, sizes[c] * DH)
        here = pl.ds(starts[c] * DH, sizes[c] * DH)
        return [
            pltpu.make_async_copy(src.at[:, there], dst.at[m, :, here], in_sems.at[m, n, c])
            for n, (src, dst) in enumerate(zip(sources, (left, right)))
        ]

    def result(m, c):
        heads = pl.ds(starts[c], sizes[c])
        return pltpu.make_async_copy(total.at[m, heads], outs[m * chunks + c], out_sems.at[m, c])

    for m in range(many):
        for kind, sources in ((1, (k_hbm, v_hbm)), (0, (q_hbm, g_hbm))):

            @pl.when(tables[m][0] == kind)
            def _():
                for c in range(chunks):
                    for copy in copies(m, c, sources):
                        copy.start()

    fill_scale(pack, d, None, sign_ref)
    for m in range(many):
        forward = tables[m][0] == 1
        for b in range(NB):
            rows = pl.ds(b * BLK, BLK)
            takes = pick(seg(d * NB + b), tables[m][1:]).astype(F32)
            weight_ref[m, rows, :] = jnp.where(forward, 1.0, sign_ref[rows, :]) * takes
    for m in range(many):
        for c in range(chunks):
            for copy in copies(m, c, (k_hbm, v_hbm)):
                copy.wait()
            for h in range(starts[c], starts[c] + sizes[c]):
                cols = pl.ds(h * DH, DH)
                rows = weighted(right[m, :, cols], weight_ref[m])
                total[m, h] = contract_rows(left[m, :, cols], rows)
            result(m, c).start()
    for m in range(many):
        for c in range(chunks):
            result(m, c).wait()


def local_sums(messages, first, sizes, scalars, tokens, after, limit):
    rows, heads, many = tokens[0].shape[0], sum(sizes), len(messages)
    out = pl.pallas_call(
        functools.partial(sums_kernel, messages, first, sizes),
        out_shape=[
            jax.ShapeDtypeStruct((size, DH, DH), F32) for _ in messages for size in sizes
        ],
        in_specs=[SMEM, SMEM] + [HBM] * 4 + [ANY],
        out_specs=[ANY] * (many * len(sizes)),
        scratch_shapes=[
            pltpu.VMEM((many, rows, heads * DH), BF16),
            pltpu.VMEM((many, rows, heads * DH), BF16),
            pltpu.VMEM((many, heads, DH, DH), F32),
            pltpu.VMEM((many, rows, DH), F32),
            pltpu.VMEM((rows, DH), F32),
            pltpu.SemaphoreType.DMA((many, 2, len(sizes))),
            pltpu.SemaphoreType.DMA((many, len(sizes))),
        ],
        compiler_params=pltpu.CompilerParams(vmem_limit_bytes=limit),
        cost_estimate=SHORT,
        name="local_sums",
    )(*scalars, *tokens, after)
    return [out[m * len(sizes) : (m + 1) * len(sizes)] for m in range(many)]


def join_kernel(message, pack, place, got_ref, own_ref, after, out_ref):
    keep = message(pack, place[0], NB)[0] == 1

    @pl.when(keep)
    def _():
        out_ref[...] = got_ref[...] + own_ref[...]

    @pl.when(jnp.logical_not(keep))
    def _():
        out_ref[...] = own_ref[...]


def join(message, scalars, got, own, after):
    block = pl.BlockSpec(got.shape, lambda i: (0, 0, 0))
    return pl.pallas_call(
        functools.partial(join_kernel, message),
        out_shape=jax.ShapeDtypeStruct(got.shape, F32),
        grid=(1,),
        in_specs=[SMEM, SMEM, block, block, ANY],
        out_specs=block,
        compiler_params=pltpu.CompilerParams(vmem_limit_bytes=JOIN_LIMIT),
        cost_estimate=SHORT,
        name="join",
    )(*scalars, got, own, after)


def inside_kernel(per, pack, place, q_ref, k_ref, v_ref, g_ref, *refs):
    o1, o2, o3, o4, mask_ref, sign_ref = refs[-6:]
    d = place[0]
    half = GROUP // 2

    @pl.when(pl.program_id(0) == 0)
    def _():
        fill_scale(pack, d, None, sign_ref)
        seg, _, _ = edges(pack, NB)
        segs = [seg(d * NB + b) for b in range(NB)]
        tri = lax.broadcasted_iota(jnp.int32, (BLK, BLK), 0) >= lax.broadcasted_iota(
            jnp.int32, (BLK, BLK), 1
        )
        for t in range(NB):
            for s in range(NB):
                if s > t:
                    tile = jnp.zeros((BLK, BLK), F32)
                elif s == t:
                    tile = jnp.where(tri, 1.0, 0.0)
                else:
                    sees = either(flag(segs[t] == segs[s]), flag(segs[s] == 0))
                    tile = jnp.full((BLK, BLK), sees.astype(F32))
                mask_ref[pl.ds(t * BLK, BLK), pl.ds(s * BLK, BLK)] = tile.astype(BF16)

    lo, hi, whole = slice(0, half), slice(half, GROUP), slice(0, GROUP)
    for h in range(per):
        cols = slice(h * DH, (h + 1) * DH)
        q, k, v = q_ref[:, cols], k_ref[:, cols], v_ref[:, cols]
        g = weighted(g_ref[:, cols], sign_ref[...])

        def masked(a, b, rows, keys):
            return contract_cols(a[rows], b[keys]).astype(BF16) * mask_ref[rows, keys]

        def put(ref, rows, value):
            ref[rows, cols] = value.astype(ref.dtype)

        s_lo = masked(q, k, lo, lo)
        s_hi = masked(q, k, hi, whole)
        put(o1, lo, plain(s_lo, v[lo]))
        put(o1, hi, plain(s_hi, v))
        gv = contract_rows(s_hi, g[hi])
        put(o4, lo, gv[lo] + contract_rows(s_lo, g[lo]))
        put(o4, hi, gv[hi])
        b_lo = masked(g, v, lo, lo)
        b_hi = masked(g, v, hi, whole)
        put(o2, lo, plain(b_lo, k[lo]))
        put(o2, hi, plain(b_hi, k))
        gk = contract_rows(b_hi, q[hi])
        put(o3, lo, gk[lo] + contract_rows(b_lo, q[lo]))
        put(o3, hi, gk[hi])


def inside_products(first, heads, scalars, tokens, before, after):
    rows, cols = tokens[0].shape
    per = 2 if first % 2 == 0 and heads % 2 == 0 else 1
    spec = pl.BlockSpec((rows, per * DH), lambda i: (0, first // per + i))
    operands = [*scalars, *tokens, after]
    specs = [SMEM, SMEM] + [spec] * 4 + [ANY]
    aliases = {}
    if before is not None:
        aliases = {len(operands) + n: n for n in range(4)}
        operands += list(before)
        specs += [ANY] * 4
    return pl.pallas_call(
        functools.partial(inside_kernel, per),
        out_shape=[jax.ShapeDtypeStruct((rows, cols), HELD)] * 4,
        grid=(heads // per,),
        in_specs=specs,
        out_specs=[spec] * 4,
        scratch_shapes=[pltpu.VMEM((rows, rows), BF16), pltpu.VMEM((rows, DH), F32)],
        input_output_aliases=aliases,
        compiler_params=pltpu.CompilerParams(vmem_limit_bytes=IN_LIMIT),
        cost_estimate=SHORT,
        name="inside_products",
    )(*operands)


def final_kernel(per, pack, place, *refs):
    q_ref, k_ref, v_ref, g_ref, i1, i2, i3, i4, r1, r2, r3 = refs[:11]
    o1, o2, o3, o4, scale_ref, sign_ref, st_ref, bk_ref = refs[-8:]
    d = place[0]

    @pl.when(pl.program_id(0) == 0)
    def _():
        fill_scale(pack, d, scale_ref, sign_ref)

    seg, _, _ = edges(pack, NB)
    forward, backward = state_table(pack, d, NB)
    for h in range(per):
        cols = slice(h * DH, (h + 1) * DH)
        got = [r1[h], r2[h], r3[h]]
        for x in range(3):
            for table, out in ((forward, st_ref), (backward, bk_ref)):
                total = None
                for weight, part in zip(table[x], got):
                    term = weight.astype(F32) * part
                    total = term if total is None else total + term
                out[x] = total.astype(BF16)
        for b in range(NB):
            rows = pl.ds(b * BLK, BLK)
            s = seg(d * NB + b)
            st, bk = st_ref[s], bk_ref[s]
            q, k, v = q_ref[rows, cols], k_ref[rows, cols], v_ref[rows, cols]
            g = weighted(g_ref[rows, cols], sign_ref[rows, :])

            def put(ref, held, value, scale=None):
                total = held[rows, cols].astype(F32) + value
                ref[rows, cols] = (total if scale is None else scale * total).astype(BF16)

            put(o1, i1, plain(q, st), scale_ref[rows, :])
            put(o2, i2, contract_cols(g, st))
            put(o3, i3, contract_cols(v, bk))
            put(o4, i4, plain(k, bk))


def final_products(first, heads, scalars, tokens, inside, got, before):
    rows, cols = tokens[0].shape
    per = 2 if first % 2 == 0 and heads % 2 == 0 else 1
    spec = pl.BlockSpec((rows, per * DH), lambda i: (0, first // per + i))
    state = pl.BlockSpec((per, DH, DH), lambda i: (i, 0, 0))
    operands = [*scalars, *tokens, *inside, *got]
    specs = [SMEM, SMEM] + [spec] * 8 + [state] * 3
    aliases = {}
    if before is not None:
        aliases = {len(operands) + n: n for n in range(4)}
        operands += list(before)
        specs += [ANY] * 4
    return pl.pallas_call(
        functools.partial(final_kernel, per),
        out_shape=[jax.ShapeDtypeStruct((rows, cols), BF16)] * 4,
        grid=(heads // per,),
        in_specs=specs,
        out_specs=[spec] * 4,
        scratch_shapes=[
            pltpu.VMEM((rows, DH), F32),
            pltpu.VMEM((rows, DH), F32),
            pltpu.VMEM((3, DH, DH), BF16),
            pltpu.VMEM((3, DH, DH), BF16),
        ],
        input_output_aliases=aliases,
        compiler_params=pltpu.CompilerParams(vmem_limit_bytes=END_LIMIT),
        cost_estimate=SHORT,
        name="final_products",
    )(*operands)


def exchange_body(queries, key_rows, value_rows, grad_out, packing):
    place = lax.axis_index("seq").astype(jnp.int32).reshape(1)
    scalars = (packing, place)
    tokens = (queries, key_rows, value_rows, grad_out)
    starts = [sum(SIZES[:c]) for c in range(len(SIZES))]
    near = [(i, i ^ 1) for i in range(4)]
    across = [(i, 3 - i) for i in range(4)]

    count = len(SIZES)
    one, two, three = [None] * count, [None] * count, [None] * count
    early = local_sums((message_one,), 0, SIZES[:1], scalars, tokens, packing, FIRST_LIMIT)[0]
    last = early[0]
    inside, out = None, None
    for what, c in ORDER:
        if what == "one":
            one[c] = lax.ppermute(early[c], "seq", near)
        elif what == "early":
            early += local_sums(
                (message_one,), SIZES[0], SIZES[1:], scalars, tokens, last, SUMS_LIMIT
            )[0]
            last = early[-1]
        elif what == "own":
            own_two, own_three = local_sums(
                (message_two, message_three), 0, SIZES, scalars, tokens, last, SUMS_LIMIT
            )
            last = own_two[0]
        elif what == "own_two":
            (own_two,) = local_sums((message_two,), 0, SIZES, scalars, tokens, last, SUMS_LIMIT)
            last = own_two[0]
        elif what == "own_three":
            (own_three,) = local_sums(
                (message_three,), 0, SIZES, scalars, tokens, last, SUMS_LIMIT
            )
            last = own_three[0]
        elif what == "two":
            last = join(message_two, scalars, one[c], own_two[c], last)
            two[c] = lax.ppermute(last, "seq", across)
        elif what == "three":
            last = join(message_three, scalars, two[c], own_three[c], last)
            three[c] = lax.ppermute(last, "seq", near)
        elif what == "in":
            first = 0 if inside is None else sum(IN_SIZES[:c])
            inside = inside_products(first, IN_SIZES[c], scalars, tokens, inside, last)
            last = inside[0]
        else:
            got = (one[c], two[c], three[c])
            out = final_products(starts[c], SIZES[c], scalars, tokens, inside, got, out)
            last = out[0]
    return tuple(out)


highest = lax.Precision.HIGHEST


def carried_in(value, axis, combine, identity, reverse):
    length, index = (lax.axis_size(axis), lax.axis_index(axis))
    everything = jax.tree.map(lambda part: lax.all_gather(part, axis), value)
    start = jax.tree.map(
        lambda part, zero: jnp.broadcast_to(jnp.asarray(zero, part.dtype), part.shape),
        value,
        identity,
    )

    def turn(k, before):
        at = length - 1 - k if reverse else k
        reached = at > index if reverse else at < index
        new = combine(before, jax.tree.map(lambda part: part[at], everything))
        return jax.tree.map(lambda a, b: jnp.where(reached, a, b), new, before)

    return lax.fori_loop(0, length, turn, start)


def block_info(packing, first_block, block_count):
    seg_starts = packing[:, 0]
    seg_ends = packing[:, 1]
    pair_col = packing[:, 2]
    role_col = packing[:, 3]
    blocks = first_block + jnp.arange(block_count, dtype=jnp.int32)
    segment = jnp.sum((seg_starts[None, :] <= blocks[:, None]).astype(jnp.int32), axis=1) - 1
    seg_ranks = jnp.arange(seg_starts.shape[0], dtype=jnp.int32)
    select = segment[:, None] == seg_ranks[None, :]
    block_role = jnp.sum(jnp.where(select, role_col[None, :], 0), axis=1)
    block_pair = jnp.sum(jnp.where(select, pair_col[None, :], 0), axis=1)
    opening = jnp.sum(jnp.where(select, seg_starts[None, :], 0), axis=1)
    prompt_sel = (segment // 3 * 3)[:, None] == seg_ranks[None, :]
    prompt_len = jnp.sum(jnp.where(prompt_sel, (seg_ends - seg_starts)[None, :], 0), axis=1)
    position = (blocks - opening)[:, None] * BLK + jnp.arange(BLK, dtype=jnp.int32)[None, :]
    visible = position + 1 + jnp.where(block_role != 0, prompt_len * BLK, 0)[:, None]
    tok_scale = lax.rsqrt((visible * DH).astype(jnp.float32))
    return (segment, block_role, block_pair, tok_scale)


def link_combine(before, behind):
    back_a, open_a, state_a = before
    back_b, open_b, state_b = behind
    empty_b = open_b < 0.0
    joins = (back_b == open_b) & (open_a == back_b) | empty_b
    state = state_b + jnp.where(joins, state_a, jnp.zeros_like(state_a))
    back_id = jnp.where(open_a < 0.0, back_b, back_a)
    open_id = jnp.where(empty_b, open_a, open_b)
    return (back_id, open_id, state)


def pick_state(carry_open, carry_state, block_ids, allowed):
    chosen = (carry_open == block_ids.astype(jnp.float32)) & allowed
    return jnp.where(chosen[:, None, None, None], carry_state[None], 0.0)


def masked_sum(flags, states):
    return jnp.einsum("j,jhde->hde", flags.astype(jnp.float32), states, precision=highest)


def split_state(state):
    upper = state.astype(jnp.bfloat16)
    upper_wide = lax.optimization_barrier(upper).astype(jnp.float32)
    lower = (state - upper_wide).astype(jnp.bfloat16)
    return (upper, lower)


def state_product(form, token_rows, parts):
    first = jnp.einsum(form, token_rows, parts[0], preferred_element_type=jnp.float32)
    return first + jnp.einsum(form, token_rows, parts[1], preferred_element_type=jnp.float32)


def body(queries, key_rows, value_rows, grad_out, packing):
    block_count = queries.shape[0] // BLK
    local_heads = queries.shape[1] // DH
    group_count = queries.shape[0] // GROUP
    final_index = block_count - 1
    first_block = lax.axis_index("seq") * block_count
    segment, block_role, block_pair, tok_scale = block_info(packing, first_block, block_count)
    dpo_sign = jnp.where(block_role == 2, -1.0, 1.0).astype(jnp.float32)
    q_blocks = queries.reshape(block_count, BLK, local_heads, DH)
    k_blocks = key_rows.reshape(block_count, BLK, local_heads, DH)
    v_blocks = value_rows.reshape(block_count, BLK, local_heads, DH)
    weight = (dpo_sign[:, None] * tok_scale)[:, :, None, None]
    g_blocks = (
        weight * grad_out.reshape(block_count, BLK, local_heads, DH).astype(jnp.float32)
    ).astype(jnp.bfloat16)
    block_kv = jnp.einsum("bshd,bshe->bhde", k_blocks, v_blocks, preferred_element_type=jnp.float32)
    block_qg = jnp.einsum("bshd,bshe->bhde", q_blocks, g_blocks, preferred_element_type=jnp.float32)
    group_of = jnp.arange(block_count, dtype=jnp.int32) // (GROUP // BLK)
    same_seg = segment[:, None] == segment[None, :]
    link = same_seg & (group_of[None, :] < group_of[:, None])
    seg_first = segment[0].astype(jnp.float32)
    seg_last = segment[final_index].astype(jnp.float32)
    neutral = jnp.full((), -1.0, jnp.float32)
    zero_state = jnp.zeros((local_heads, DH, DH), jnp.float32)
    is_prompt = block_role == 0
    is_reply = block_role != 0
    pair_count = packing.shape[0] // 3
    pair_hot = (block_pair[:, None] == jnp.arange(pair_count, dtype=jnp.int32)[None, :]).astype(
        jnp.float32
    )
    fwd_seg = masked_sum(segment == segment[final_index], block_kv)
    carried = carried_in(
        (seg_first, seg_last, fwd_seg), "seq", link_combine, (neutral, neutral, zero_state), False
    )
    prompt_part = jnp.einsum(
        "jp,jhde->phde",
        pair_hot * is_prompt[:, None].astype(jnp.float32),
        block_kv,
        precision=highest,
    )
    prompt_all = lax.psum(prompt_part, "seq")
    outside_in = pick_state(carried[1], carried[2], segment, is_reply | is_prompt)
    outside_in = outside_in + jnp.einsum(
        "bp,phde->bhde",
        pair_hot * is_reply[:, None].astype(jnp.float32),
        prompt_all,
        precision=highest,
    )
    rev_seg = masked_sum(segment == segment[0], block_qg)
    returned = carried_in(
        (seg_last, seg_first, rev_seg), "seq", link_combine, (neutral, neutral, zero_state), True
    )
    reply_part = jnp.einsum(
        "jp,jhde->phde",
        pair_hot * is_reply[:, None].astype(jnp.float32),
        block_qg,
        precision=highest,
    )
    reply_all = lax.psum(reply_part, "seq")
    outside_back = pick_state(returned[1], returned[2], segment, is_reply | is_prompt)
    outside_back = outside_back + jnp.einsum(
        "bp,phde->bhde",
        pair_hot * is_prompt[:, None].astype(jnp.float32),
        reply_all,
        precision=highest,
    )
    link_f = link.astype(jnp.float32)
    state = jnp.einsum("bj,jhde->bhde", link_f, block_kv, precision=highest) + outside_in
    back_state = jnp.einsum("bj,bhde->jhde", link_f, block_qg, precision=highest) + outside_back
    state_parts = split_state(state)
    back_parts = split_state(back_state)
    tok_seg = jnp.repeat(segment, BLK).reshape(group_count, GROUP)
    places = jnp.arange(GROUP, dtype=jnp.int32)
    causal = (tok_seg[:, :, None] == tok_seg[:, None, :]) & (
        places[None, :, None] >= places[None, None, :]
    )
    q_groups = queries.reshape(group_count, GROUP, local_heads, DH)
    k_groups = key_rows.reshape(group_count, GROUP, local_heads, DH)
    v_groups = value_rows.reshape(group_count, GROUP, local_heads, DH)
    g_groups = g_blocks.reshape(group_count, GROUP, local_heads, DH)
    scores = jnp.einsum("cshd,cthd->chst", q_groups, k_groups, preferred_element_type=jnp.float32)
    attn_weights = jnp.where(causal[:, None], scores, 0.0).astype(jnp.bfloat16)
    inside = jnp.einsum(
        "chst,cthd->cshd", attn_weights, v_groups, preferred_element_type=jnp.float32
    )
    inside = inside.reshape(block_count, BLK, local_heads, DH)
    outside = state_product("bshd,bhde->bshe", q_blocks, state_parts)
    attended = (tok_scale[:, :, None, None] * (inside + outside)).astype(jnp.bfloat16)
    back_raw = jnp.einsum("cshd,cthd->chst", g_groups, v_groups, preferred_element_type=jnp.float32)
    back_weights = jnp.where(causal[:, None], back_raw, 0.0).astype(jnp.bfloat16)
    grad_q = jnp.einsum(
        "chst,cthd->cshd", back_weights, k_groups, preferred_element_type=jnp.float32
    )
    grad_q = grad_q.reshape(block_count, BLK, local_heads, DH)
    grad_q = grad_q + state_product("bshe,bhde->bshd", g_blocks, state_parts)
    grad_k = jnp.einsum(
        "chst,cshd->cthd", back_weights, q_groups, preferred_element_type=jnp.float32
    )
    grad_k = grad_k.reshape(block_count, BLK, local_heads, DH)
    grad_k = grad_k + state_product("bshe,bhde->bshd", v_blocks, back_parts)
    grad_v = jnp.einsum(
        "chst,cshd->cthd", attn_weights, g_groups, preferred_element_type=jnp.float32
    )
    grad_v = grad_v.reshape(block_count, BLK, local_heads, DH)
    grad_v = grad_v + state_product("bshd,bhde->bshe", k_blocks, back_parts)
    rows = queries.shape[0]
    columns = queries.shape[1]
    return (
        attended.reshape(rows, columns),
        grad_q.astype(jnp.bfloat16).reshape(rows, columns),
        grad_k.astype(jnp.bfloat16).reshape(rows, columns),
        grad_v.astype(jnp.bfloat16).reshape(rows, columns),
    )


def solution(mesh):
    tokens = P(("grp", "seq"), "head")

    def program(queries, key_rows, value_rows, grad_out, packing):
        rows = queries.shape[0] // mesh.shape["grp"] // mesh.shape["seq"]
        heads = queries.shape[1] // mesh.shape["head"] // DH
        pairs = packing.shape[0] // mesh.shape["grp"] // 3
        four = mesh.shape["seq"] == 4 and pairs == 1
        fits = rows == GROUP and heads == sum(SIZES)
        return jax.shard_map(
            exchange_body if four and fits else body,
            mesh=mesh,
            in_specs=(tokens,) * 4 + (P("grp", None),),
            out_specs=(tokens,) * 4,
            check_vma=False,
        )(queries, key_rows, value_rows, grad_out, packing)

    return program
```

```python
import functools

import jax
import jax.numpy as jnp
from jax import lax
from jax.experimental import pallas as pl
from jax.experimental.pallas import tpu as pltpu
from jax.sharding import PartitionSpec as P

DH = 128
BLK = 128
GROUP = 512
NB = GROUP // BLK
SIZES = (4, 4)
IN_SIZES = (4, 4)
ORDER = (
    ("one", 0),
    ("own_two", 0),
    ("early", 0),
    ("one", 1),
    ("two", 0),
    ("own_three", 0),
    ("in", 0),
    ("two", 1),
    ("in", 1),
    ("three", 0),
    ("base", 0),
    ("three", 1),
    ("base", 1),
    ("end", 0),
    ("end", 1),
)
MIB = 2**20
FIRST_LIMIT = 60 * MIB
SUMS_LIMIT = 12 * MIB
JOIN_LIMIT = 4 * MIB
IN_LIMIT = 16 * MIB
END_LIMIT = 16 * MIB
HELD = jnp.bfloat16
F32 = jnp.float32
BF16 = jnp.bfloat16


def flag(condition):
    return jnp.where(condition, 1, 0).astype(jnp.int32)


def either(*flags):
    out = flags[0]
    for f in flags[1:]:
        out = jnp.maximum(out, f)
    return out


def pick(index, choices):
    out = jnp.int32(0) + choices[-1]
    for n in range(len(choices) - 2, -1, -1):
        out = jnp.where(index == n, choices[n], out)
    return out


def pick_rows(index, rows):
    return [pick(index, [row[c] for row in rows]) for c in range(len(rows[0]))]


def edges(pack, blocks):
    one, two = pack[1, 0], pack[2, 0]

    def seg(b):
        return flag(b >= one) + flag(b >= two)

    first = [seg(blocks * i) for i in range(4)]
    last = [seg(blocks * i + blocks - 1) for i in range(4)]
    return seg, first, last


def message_one(pack, d, blocks):
    _, f, l = edges(pack, blocks)
    every = either(flag(l[2] == 0), flag(l[2] == 1) * flag(l[1] == 0))
    at_p, from_p = flag(l[0] == 0), flag(f[2] == 0)
    return pick_rows(
        d,
        [
            [1, 1, flag(f[2] == 1), flag(f[2] == 2)],
            [at_p, at_p, 0, 1 - at_p],
            [from_p, 0, from_p * flag(f[3] == 1), from_p * flag(f[3] == 2) + 1 - from_p],
            [0, every, either(every, flag(l[2] == 1)), either(every, flag(l[2] == 2))],
        ],
    )


def message_two(pack, d, blocks):
    _, f, l = edges(pack, blocks)
    return pick_rows(
        d,
        [
            [flag(l[0] == 0), 1, 1, 0, 0],
            [1, 1, 1, flag(f[2] == 1), flag(f[2] == 2)],
            [
                1 - flag(l[1] == 1) * flag(l[2] == 2),
                0,
                flag(l[1] == 0),
                flag(l[1] <= 1),
                flag(l[1] != 1),
            ],
            [flag(f[2] != 0), 0, 0, 0, 1],
        ],
    )


def message_three(pack, d, blocks):
    _, f, l = edges(pack, blocks)
    from_p, at_p, first_p = flag(f[2] == 0), flag(l[1] == 0), flag(f[1] == 0)
    return pick_rows(
        d,
        [
            [first_p, 1, 0, 1 - first_p, 0],
            [
                1 - flag(l[0] == 1) * flag(l[1] == 2),
                0,
                flag(l[0] == 0),
                flag(l[0] <= 1),
                flag(l[0] != 1),
            ],
            [
                either(from_p, flag(f[2] == f[3])),
                1,
                from_p,
                (1 - from_p) * flag(f[3] == 1),
                (1 - from_p) * flag(f[3] == 2),
            ],
            [1 - at_p, 0, 0, at_p, 0],
        ],
    )


def state_table(pack, d, blocks):
    _, f, l = edges(pack, blocks)
    apart = flag(f[2] == 1) * flag(l[1] != 0)
    from_p = flag(f[2] == 0)
    crossing = (1 - from_p) * flag(f[3] == 1)
    forward = [
        pick_rows(d, [[0, 0, 0], [1, 0, 0], [0, 1, 0], [0, 0, 1]]),
        pick_rows(
            d,
            [
                [0, 0, 0],
                [1, 0, flag(f[1] == 1) * flag(f[2] == 2)],
                [0, 1, 0],
                [from_p * flag(f[3] == 1), 0, 1],
            ],
        ),
        pick_rows(
            d,
            [
                [0, 0, 0],
                [1, 0, 0],
                [0, 1 - apart, apart],
                [
                    from_p * flag(f[3] == 2),
                    either(crossing, (1 - from_p) * flag(f[2] != f[3])),
                    1 - crossing,
                ],
            ],
        ),
    ]
    backward = [
        pick_rows(
            d,
            [
                [
                    flag(l[0] == 1),
                    either(flag(l[0] == 1), flag(l[0] == 0) * flag(l[1] == 1)),
                    1,
                ],
                [0, 1, flag(l[1] == 1)],
                [1, 0, 0],
                [0, 0, 0],
            ],
        ),
        pick_rows(
            d,
            [
                [0, 0, flag(l[0] == 1)],
                [0, flag(l[1] == 1), 0],
                [flag(l[2] == 1) * flag(l[1] != 0), 0, flag(l[2] == 1) * flag(l[1] == 0)],
                [0, 0, 0],
            ],
        ),
        pick_rows(
            d,
            [
                [0, 0, flag(l[0] == 2)],
                [0, flag(l[1] == 2), 0],
                [flag(l[2] == 2), 0, 0],
                [0, 0, 0],
            ],
        ),
    ]
    return forward, backward


SHORT = pl.CostEstimate(flops=1, bytes_accessed=1, transcendentals=0)
SMEM = pl.BlockSpec(memory_space=pltpu.SMEM)
ANY = pl.BlockSpec(memory_space=pl.ANY)
HBM = pl.BlockSpec(memory_space=pltpu.HBM)
VMEM = pl.BlockSpec(memory_space=pltpu.VMEM)


def order_spec(after):
    return SMEM if after.dtype == jnp.int32 else ANY


def fill_scale(pack, d, scale_ref, sign_ref):
    seg, _, _ = edges(pack, NB)
    prompt = pack[0, 1] - pack[0, 0]
    for b in range(NB):
        block = d * NB + b
        s = seg(block)
        start = pick(s, [pack[0, 0], pack[1, 0], pack[2, 0]])
        role = pick(s, [pack[0, 3], pack[1, 3], pack[2, 3]])
        base = (block - start) * BLK + 1 + jnp.where(role != 0, prompt * BLK, 0)
        seen = base + lax.broadcasted_iota(jnp.int32, (BLK, DH), 0)
        scale = lax.rsqrt((seen * DH).astype(F32))
        rows = pl.ds(b * BLK, BLK)
        if scale_ref is not None:
            scale_ref[rows, :] = scale
        sign_ref[rows, :] = jnp.where(role == 2, -1.0, 1.0) * scale


def weighted(rows, weight):
    return (rows.astype(F32) * weight).astype(BF16)


def contract_rows(a, b):
    return lax.dot_general(a, b, (((0,), (0,)), ((), ())), preferred_element_type=F32)


def contract_cols(a, b):
    return lax.dot_general(a, b, (((1,), (1,)), ((), ())), preferred_element_type=F32)


def plain(a, b):
    return lax.dot_general(a, b, (((1,), (0,)), ((), ())), preferred_element_type=F32)


def sums_kernel(messages, first, sizes, pack, place, q_hbm, k_hbm, v_hbm, g_hbm, after, *refs):
    many, chunks = len(messages), len(sizes)
    outs = refs[: many * chunks]
    left, right, total, weight_ref, sign_ref, in_sems, out_sems = refs[many * chunks :]
    d = place[0]
    seg, _, _ = edges(pack, NB)
    tables = [m(pack, d, NB)[-4:] for m in messages]
    starts = [sum(sizes[:c]) for c in range(chunks)]

    def copies(m, c, sources):
        there = pl.ds((first + starts[c]) * DH, sizes[c] * DH)
        here = pl.ds(starts[c] * DH, sizes[c] * DH)
        return [
            pltpu.make_async_copy(src.at[:, there], dst.at[m, :, here], in_sems.at[m, n, c])
            for n, (src, dst) in enumerate(zip(sources, (left, right)))
        ]

    def result(m, c):
        heads = pl.ds(starts[c], sizes[c])
        return pltpu.make_async_copy(total.at[m, heads], outs[m * chunks + c], out_sems.at[m, c])

    for m in range(many):
        for kind, sources in ((1, (k_hbm, v_hbm)), (0, (q_hbm, g_hbm))):

            @pl.when(tables[m][0] == kind)
            def _():
                for c in range(chunks):
                    for copy in copies(m, c, sources):
                        copy.start()

    fill_scale(pack, d, None, sign_ref)
    for m in range(many):
        forward = tables[m][0] == 1
        for b in range(NB):
            rows = pl.ds(b * BLK, BLK)
            takes = pick(seg(d * NB + b), tables[m][1:]).astype(F32)
            weight_ref[m, rows, :] = jnp.where(forward, 1.0, sign_ref[rows, :]) * takes
    for m in range(many):
        for c in range(chunks):
            for copy in copies(m, c, (k_hbm, v_hbm)):
                copy.wait()
            for h in range(starts[c], starts[c] + sizes[c]):
                cols = pl.ds(h * DH, DH)
                rows = weighted(right[m, :, cols], weight_ref[m])
                total[m, h] = contract_rows(left[m, :, cols], rows)
            result(m, c).start()
    for m in range(many):
        for c in range(chunks):
            result(m, c).wait()


def local_sums(messages, first, sizes, scalars, tokens, after, limit):
    rows, heads, many = tokens[0].shape[0], sum(sizes), len(messages)
    out = pl.pallas_call(
        functools.partial(sums_kernel, messages, first, sizes),
        out_shape=[
            jax.ShapeDtypeStruct((size, DH, DH), F32) for _ in messages for size in sizes
        ],
        in_specs=[SMEM, SMEM] + [HBM] * 4 + [ANY],
        out_specs=[ANY] * (many * len(sizes)),
        scratch_shapes=[
            pltpu.VMEM((many, rows, heads * DH), BF16),
            pltpu.VMEM((many, rows, heads * DH), BF16),
            pltpu.VMEM((many, heads, DH, DH), F32),
            pltpu.VMEM((many, rows, DH), F32),
            pltpu.VMEM((rows, DH), F32),
            pltpu.SemaphoreType.DMA((many, 2, len(sizes))),
            pltpu.SemaphoreType.DMA((many, len(sizes))),
        ],
        compiler_params=pltpu.CompilerParams(vmem_limit_bytes=limit),
        cost_estimate=SHORT,
        name="local_sums",
    )(*scalars, *tokens, after)
    return [out[m * len(sizes) : (m + 1) * len(sizes)] for m in range(many)]


def join_kernel(message, pack, place, got_ref, own_ref, after, out_ref):
    keep = message(pack, place[0], NB)[0] == 1

    @pl.when(keep)
    def _():
        out_ref[...] = got_ref[...] + own_ref[...]

    @pl.when(jnp.logical_not(keep))
    def _():
        out_ref[...] = own_ref[...]


def join(message, scalars, got, own, after):
    block = pl.BlockSpec(got.shape, lambda i: (0, 0, 0))
    return pl.pallas_call(
        functools.partial(join_kernel, message),
        out_shape=jax.ShapeDtypeStruct(got.shape, F32),
        grid=(1,),
        in_specs=[SMEM, SMEM, block, block, order_spec(after)],
        out_specs=block,
        compiler_params=pltpu.CompilerParams(vmem_limit_bytes=JOIN_LIMIT),
        cost_estimate=SHORT,
        name="join",
    )(*scalars, got, own, after)


def inside_kernel(per, pack, place, q_ref, k_ref, v_ref, g_ref, *refs):
    o1, o2, o3, o4, mask_ref, sign_ref = refs[-6:]
    d = place[0]
    half = GROUP // 2

    @pl.when(pl.program_id(0) == 0)
    def _():
        fill_scale(pack, d, None, sign_ref)
        seg, _, _ = edges(pack, NB)
        segs = [seg(d * NB + b) for b in range(NB)]
        tri = lax.broadcasted_iota(jnp.int32, (BLK, BLK), 0) >= lax.broadcasted_iota(
            jnp.int32, (BLK, BLK), 1
        )
        for t in range(NB):
            for s in range(NB):
                if s > t:
                    tile = jnp.zeros((BLK, BLK), F32)
                elif s == t:
                    tile = jnp.where(tri, 1.0, 0.0)
                else:
                    sees = either(flag(segs[t] == segs[s]), flag(segs[s] == 0))
                    tile = jnp.full((BLK, BLK), sees.astype(F32))
                mask_ref[pl.ds(t * BLK, BLK), pl.ds(s * BLK, BLK)] = tile.astype(BF16)

    lo, hi, whole = slice(0, half), slice(half, GROUP), slice(0, GROUP)
    for h in range(per):
        cols = slice(h * DH, (h + 1) * DH)
        q, k, v = q_ref[:, cols], k_ref[:, cols], v_ref[:, cols]
        g = weighted(g_ref[:, cols], sign_ref[...])

        def masked(a, b, rows, keys):
            return contract_cols(a[rows], b[keys]).astype(BF16) * mask_ref[rows, keys]

        def put(ref, rows, value):
            ref[rows, cols] = value.astype(ref.dtype)

        s_lo = masked(q, k, lo, lo)
        s_hi = masked(q, k, hi, whole)
        put(o1, lo, plain(s_lo, v[lo]))
        put(o1, hi, plain(s_hi, v))
        gv = contract_rows(s_hi, g[hi])
        put(o4, lo, gv[lo] + contract_rows(s_lo, g[lo]))
        put(o4, hi, gv[hi])
        b_lo = masked(g, v, lo, lo)
        b_hi = masked(g, v, hi, whole)
        put(o2, lo, plain(b_lo, k[lo]))
        put(o2, hi, plain(b_hi, k))
        gk = contract_rows(b_hi, q[hi])
        put(o3, lo, gk[lo] + contract_rows(b_lo, q[lo]))
        put(o3, hi, gk[hi])


def inside_products(first, heads, scalars, tokens, before, after):
    rows, cols = tokens[0].shape
    per = 2 if first % 2 == 0 and heads % 2 == 0 else 1
    spec = pl.BlockSpec((rows, per * DH), lambda i: (0, first // per + i))
    operands = [*scalars, *tokens, after]
    specs = [SMEM, SMEM] + [spec] * 4 + [order_spec(after)]
    aliases = {}
    if before is not None:
        aliases = {len(operands) + n: n for n in range(4)}
        operands += list(before)
        specs += [ANY] * 4
    return pl.pallas_call(
        functools.partial(inside_kernel, per),
        out_shape=[jax.ShapeDtypeStruct((rows, cols), HELD)] * 4,
        grid=(heads // per,),
        in_specs=specs,
        out_specs=[spec] * 4,
        scratch_shapes=[pltpu.VMEM((rows, rows), BF16), pltpu.VMEM((rows, DH), F32)],
        input_output_aliases=aliases,
        compiler_params=pltpu.CompilerParams(vmem_limit_bytes=IN_LIMIT),
        cost_estimate=SHORT,
        name="inside_products",
    )(*operands)


def base_kernel(first, heads, pack, place, *refs):
    q_ref, k_ref, v_ref, g_ref, i1, i2, i3, i4, r1, r2, _ = refs[:11]
    o1, o2, o3, o4, sign_ref, both_ref = refs[11:]
    d = place[0]
    fill_scale(pack, d, None, sign_ref)
    seg, _, _ = edges(pack, NB)
    segs = [seg(d * NB + b) for b in range(NB)]
    tables = state_table(pack, d, NB)
    weights = [[[w.astype(F32) for w in row] for row in table] for table in tables]
    both_ref[...] = jnp.zeros_like(both_ref)
    for h in range(heads):
        here = slice(h * DH, (h + 1) * DH)
        cols = slice((first + h) * DH, (first + h + 1) * DH)
        for x in range(3):
            for n, table in enumerate(weights):
                total = table[x][0] * r1[h] + table[x][1] * r2[h]
                part = slice(n * DH, (n + 1) * DH)
                both_ref[h, x, part, part] = total.astype(BF16)
        for b in range(NB):
            rows = slice(b * BLK, (b + 1) * BLK)
            states = both_ref[h, segs[b]]
            q, k, v = q_ref[rows, cols], k_ref[rows, cols], v_ref[rows, cols]
            g = weighted(g_ref[rows, cols], sign_ref[rows, :])
            one = plain(jnp.concatenate([q, k], axis=1), states)
            two = contract_cols(jnp.concatenate([g, v], axis=1), states)
            o1[rows, here] = i1[rows, cols].astype(F32) + one[:, :DH]
            o4[rows, here] = i4[rows, cols].astype(F32) + one[:, DH:]
            o2[rows, here] = i2[rows, cols].astype(F32) + two[:, :DH]
            o3[rows, here] = i3[rows, cols].astype(F32) + two[:, DH:]


def base_products(first, heads, scalars, tokens, inside, got, after):
    rows = tokens[0].shape[0]
    return pl.pallas_call(
        functools.partial(base_kernel, first, heads),
        out_shape=[jax.ShapeDtypeStruct((rows, heads * DH), F32)] * 4,
        in_specs=[SMEM, SMEM] + [VMEM] * 10 + [order_spec(after)],
        out_specs=[VMEM] * 4,
        scratch_shapes=[
            pltpu.VMEM((rows, DH), F32),
            pltpu.VMEM((heads, 3, 2 * DH, 2 * DH), BF16),
        ],
        compiler_params=pltpu.CompilerParams(vmem_limit_bytes=END_LIMIT),
        cost_estimate=SHORT,
        name="base_products",
    )(*scalars, *tokens, *inside, *got, after)


def final_kernel(first, heads, pack, place, *refs):
    q_ref, k_ref, v_ref, g_ref, i1, i2, i3, i4, r3 = refs[:9]
    outs = refs[-12:-8]
    b1, b2, b3, b4, scale_ref, sign_ref, both_ref, sems = refs[-8:]
    d = place[0]
    fill_scale(pack, d, scale_ref, sign_ref)
    seg, _, _ = edges(pack, NB)
    segs = [seg(d * NB + b) for b in range(NB)]
    ahead, behind = [
        [pick(s, [row[2] for row in table]).astype(F32) for s in segs]
        for table in state_table(pack, d, NB)
    ]
    both_ref[...] = jnp.zeros_like(both_ref)
    held = ((b1, outs[0]), (b2, outs[1]), (b3, outs[2]), (b4, outs[3]))

    def copies(h):
        return [
            pltpu.make_async_copy(
                buffer.at[:, pl.ds(h * DH, DH)], out.at[:, pl.ds((first + h) * DH, DH)], sems.at[n, h]
            )
            for n, (buffer, out) in enumerate(held)
        ]

    for h in range(heads):
        here = slice(h * DH, (h + 1) * DH)
        cols = slice((first + h) * DH, (first + h + 1) * DH)
        state = r3[h].astype(BF16)
        both_ref[h, :DH, :DH] = state
        both_ref[h, DH:, DH:] = state
        states = both_ref[h]
        q, k, v = q_ref[:, cols], k_ref[:, cols], v_ref[:, cols]
        g = weighted(g_ref[:, cols], sign_ref[...])
        one = plain(jnp.concatenate([q, k], axis=1), states)
        two = contract_cols(jnp.concatenate([g, v], axis=1), states)
        for b in range(NB):
            rows = slice(b * BLK, (b + 1) * BLK)
            total = i1[rows, here] + ahead[b] * one[rows, :DH]
            b1[rows, here] = (scale_ref[rows, :] * total).astype(BF16)
            b4[rows, here] = (i4[rows, here] + behind[b] * one[rows, DH:]).astype(BF16)
            b2[rows, here] = (i2[rows, here] + ahead[b] * two[rows, :DH]).astype(BF16)
            b3[rows, here] = (i3[rows, here] + behind[b] * two[rows, DH:]).astype(BF16)
        for copy in copies(h):
            copy.start()
    for h in range(heads):
        for copy in copies(h):
            copy.wait()


def final_products(first, heads, scalars, tokens, base, got, before):
    rows, cols = tokens[0].shape
    operands = [*scalars, *tokens, *base, got]
    specs = [SMEM, SMEM] + [VMEM] * 9
    aliases = {}
    if before is not None:
        aliases = {len(operands) + n: n for n in range(4)}
        operands += list(before)
        specs += [ANY] * 4
    return pl.pallas_call(
        functools.partial(final_kernel, first, heads),
        out_shape=[jax.ShapeDtypeStruct((rows, cols), BF16)] * 4,
        in_specs=specs,
        out_specs=[ANY] * 4,
        scratch_shapes=[pltpu.VMEM((rows, heads * DH), BF16)] * 4
        + [
            pltpu.VMEM((rows, DH), F32),
            pltpu.VMEM((rows, DH), F32),
            pltpu.VMEM((heads, 2 * DH, 2 * DH), BF16),
            pltpu.SemaphoreType.DMA((4, heads)),
        ],
        input_output_aliases=aliases,
        compiler_params=pltpu.CompilerParams(vmem_limit_bytes=END_LIMIT),
        cost_estimate=SHORT,
        name="final_products",
    )(*operands)


def exchange_body(queries, key_rows, value_rows, grad_out, packing):
    place = lax.axis_index("seq").astype(jnp.int32).reshape(1)
    scalars = (packing, place)
    tokens = (queries, key_rows, value_rows, grad_out)
    starts = [sum(SIZES[:c]) for c in range(len(SIZES))]
    near = [(i, i ^ 1) for i in range(4)]
    across = [(i, 3 - i) for i in range(4)]

    count = len(SIZES)
    one, two, three = [None] * count, [None] * count, [None] * count
    early = local_sums((message_one,), 0, SIZES[:1], scalars, tokens, packing, FIRST_LIMIT)[0]
    last = early[0]
    inside, out, base = None, None, [None] * count
    for what, c in ORDER:
        if what == "one":
            one[c] = lax.ppermute(early[c], "seq", near)
        elif what == "early":
            early += local_sums(
                (message_one,), SIZES[0], SIZES[1:], scalars, tokens, last, SUMS_LIMIT
            )[0]
            last = early[-1]
        elif what == "own_two":
            (own_two,) = local_sums((message_two,), 0, SIZES, scalars, tokens, last, SUMS_LIMIT)
            last = own_two[0]
        elif what == "own_three":
            (own_three,) = local_sums(
                (message_three,), 0, SIZES, scalars, tokens, last, SUMS_LIMIT
            )
            last = own_three[0]
        elif what == "base":
            got = (one[c], two[c])
            base[c] = base_products(starts[c], SIZES[c], scalars, tokens, inside, got, last)
            last = base[c][0]
        elif what == "two":
            last = join(message_two, scalars, one[c], own_two[c], last)
            two[c] = lax.ppermute(last, "seq", across)
        elif what == "three":
            last = join(message_three, scalars, two[c], own_three[c], last)
            three[c] = lax.ppermute(last, "seq", near)
        elif what == "in":
            first = 0 if inside is None else sum(IN_SIZES[:c])
            inside = inside_products(first, IN_SIZES[c], scalars, tokens, inside, last)
            last = inside[0]
        else:
            out = final_products(starts[c], SIZES[c], scalars, tokens, base[c], three[c], out)
            last = out[0]
    return tuple(out)


highest = lax.Precision.HIGHEST


def carried_in(value, axis, combine, identity, reverse):
    length, index = (lax.axis_size(axis), lax.axis_index(axis))
    everything = jax.tree.map(lambda part: lax.all_gather(part, axis), value)
    start = jax.tree.map(
        lambda part, zero: jnp.broadcast_to(jnp.asarray(zero, part.dtype), part.shape),
        value,
        identity,
    )

    def turn(k, before):
        at = length - 1 - k if reverse else k
        reached = at > index if reverse else at < index
        new = combine(before, jax.tree.map(lambda part: part[at], everything))
        return jax.tree.map(lambda a, b: jnp.where(reached, a, b), new, before)

    return lax.fori_loop(0, length, turn, start)


def block_info(packing, first_block, block_count):
    seg_starts = packing[:, 0]
    seg_ends = packing[:, 1]
    pair_col = packing[:, 2]
    role_col = packing[:, 3]
    blocks = first_block + jnp.arange(block_count, dtype=jnp.int32)
    segment = jnp.sum((seg_starts[None, :] <= blocks[:, None]).astype(jnp.int32), axis=1) - 1
    seg_ranks = jnp.arange(seg_starts.shape[0], dtype=jnp.int32)
    select = segment[:, None] == seg_ranks[None, :]
    block_role = jnp.sum(jnp.where(select, role_col[None, :], 0), axis=1)
    block_pair = jnp.sum(jnp.where(select, pair_col[None, :], 0), axis=1)
    opening = jnp.sum(jnp.where(select, seg_starts[None, :], 0), axis=1)
    prompt_sel = (segment // 3 * 3)[:, None] == seg_ranks[None, :]
    prompt_len = jnp.sum(jnp.where(prompt_sel, (seg_ends - seg_starts)[None, :], 0), axis=1)
    position = (blocks - opening)[:, None] * BLK + jnp.arange(BLK, dtype=jnp.int32)[None, :]
    visible = position + 1 + jnp.where(block_role != 0, prompt_len * BLK, 0)[:, None]
    tok_scale = lax.rsqrt((visible * DH).astype(jnp.float32))
    return (segment, block_role, block_pair, tok_scale)


def link_combine(before, behind):
    back_a, open_a, state_a = before
    back_b, open_b, state_b = behind
    empty_b = open_b < 0.0
    joins = (back_b == open_b) & (open_a == back_b) | empty_b
    state = state_b + jnp.where(joins, state_a, jnp.zeros_like(state_a))
    back_id = jnp.where(open_a < 0.0, back_b, back_a)
    open_id = jnp.where(empty_b, open_a, open_b)
    return (back_id, open_id, state)


def pick_state(carry_open, carry_state, block_ids, allowed):
    chosen = (carry_open == block_ids.astype(jnp.float32)) & allowed
    return jnp.where(chosen[:, None, None, None], carry_state[None], 0.0)


def masked_sum(flags, states):
    return jnp.einsum("j,jhde->hde", flags.astype(jnp.float32), states, precision=highest)


def split_state(state):
    upper = state.astype(jnp.bfloat16)
    upper_wide = lax.optimization_barrier(upper).astype(jnp.float32)
    lower = (state - upper_wide).astype(jnp.bfloat16)
    return (upper, lower)


def state_product(form, token_rows, parts):
    first = jnp.einsum(form, token_rows, parts[0], preferred_element_type=jnp.float32)
    return first + jnp.einsum(form, token_rows, parts[1], preferred_element_type=jnp.float32)


def body(queries, key_rows, value_rows, grad_out, packing):
    block_count = queries.shape[0] // BLK
    local_heads = queries.shape[1] // DH
    group_count = queries.shape[0] // GROUP
    final_index = block_count - 1
    first_block = lax.axis_index("seq") * block_count
    segment, block_role, block_pair, tok_scale = block_info(packing, first_block, block_count)
    dpo_sign = jnp.where(block_role == 2, -1.0, 1.0).astype(jnp.float32)
    q_blocks = queries.reshape(block_count, BLK, local_heads, DH)
    k_blocks = key_rows.reshape(block_count, BLK, local_heads, DH)
    v_blocks = value_rows.reshape(block_count, BLK, local_heads, DH)
    weight = (dpo_sign[:, None] * tok_scale)[:, :, None, None]
    g_blocks = (
        weight * grad_out.reshape(block_count, BLK, local_heads, DH).astype(jnp.float32)
    ).astype(jnp.bfloat16)
    block_kv = jnp.einsum("bshd,bshe->bhde", k_blocks, v_blocks, preferred_element_type=jnp.float32)
    block_qg = jnp.einsum("bshd,bshe->bhde", q_blocks, g_blocks, preferred_element_type=jnp.float32)
    group_of = jnp.arange(block_count, dtype=jnp.int32) // (GROUP // BLK)
    same_seg = segment[:, None] == segment[None, :]
    link = same_seg & (group_of[None, :] < group_of[:, None])
    seg_first = segment[0].astype(jnp.float32)
    seg_last = segment[final_index].astype(jnp.float32)
    neutral = jnp.full((), -1.0, jnp.float32)
    zero_state = jnp.zeros((local_heads, DH, DH), jnp.float32)
    is_prompt = block_role == 0
    is_reply = block_role != 0
    pair_count = packing.shape[0] // 3
    pair_hot = (block_pair[:, None] == jnp.arange(pair_count, dtype=jnp.int32)[None, :]).astype(
        jnp.float32
    )
    fwd_seg = masked_sum(segment == segment[final_index], block_kv)
    carried = carried_in(
        (seg_first, seg_last, fwd_seg), "seq", link_combine, (neutral, neutral, zero_state), False
    )
    prompt_part = jnp.einsum(
        "jp,jhde->phde",
        pair_hot * is_prompt[:, None].astype(jnp.float32),
        block_kv,
        precision=highest,
    )
    prompt_all = lax.psum(prompt_part, "seq")
    outside_in = pick_state(carried[1], carried[2], segment, is_reply | is_prompt)
    outside_in = outside_in + jnp.einsum(
        "bp,phde->bhde",
        pair_hot * is_reply[:, None].astype(jnp.float32),
        prompt_all,
        precision=highest,
    )
    rev_seg = masked_sum(segment == segment[0], block_qg)
    returned = carried_in(
        (seg_last, seg_first, rev_seg), "seq", link_combine, (neutral, neutral, zero_state), True
    )
    reply_part = jnp.einsum(
        "jp,jhde->phde",
        pair_hot * is_reply[:, None].astype(jnp.float32),
        block_qg,
        precision=highest,
    )
    reply_all = lax.psum(reply_part, "seq")
    outside_back = pick_state(returned[1], returned[2], segment, is_reply | is_prompt)
    outside_back = outside_back + jnp.einsum(
        "bp,phde->bhde",
        pair_hot * is_prompt[:, None].astype(jnp.float32),
        reply_all,
        precision=highest,
    )
    link_f = link.astype(jnp.float32)
    state = jnp.einsum("bj,jhde->bhde", link_f, block_kv, precision=highest) + outside_in
    back_state = jnp.einsum("bj,bhde->jhde", link_f, block_qg, precision=highest) + outside_back
    state_parts = split_state(state)
    back_parts = split_state(back_state)
    tok_seg = jnp.repeat(segment, BLK).reshape(group_count, GROUP)
    places = jnp.arange(GROUP, dtype=jnp.int32)
    causal = (tok_seg[:, :, None] == tok_seg[:, None, :]) & (
        places[None, :, None] >= places[None, None, :]
    )
    q_groups = queries.reshape(group_count, GROUP, local_heads, DH)
    k_groups = key_rows.reshape(group_count, GROUP, local_heads, DH)
    v_groups = value_rows.reshape(group_count, GROUP, local_heads, DH)
    g_groups = g_blocks.reshape(group_count, GROUP, local_heads, DH)
    scores = jnp.einsum("cshd,cthd->chst", q_groups, k_groups, preferred_element_type=jnp.float32)
    attn_weights = jnp.where(causal[:, None], scores, 0.0).astype(jnp.bfloat16)
    inside = jnp.einsum(
        "chst,cthd->cshd", attn_weights, v_groups, preferred_element_type=jnp.float32
    )
    inside = inside.reshape(block_count, BLK, local_heads, DH)
    outside = state_product("bshd,bhde->bshe", q_blocks, state_parts)
    attended = (tok_scale[:, :, None, None] * (inside + outside)).astype(jnp.bfloat16)
    back_raw = jnp.einsum("cshd,cthd->chst", g_groups, v_groups, preferred_element_type=jnp.float32)
    back_weights = jnp.where(causal[:, None], back_raw, 0.0).astype(jnp.bfloat16)
    grad_q = jnp.einsum(
        "chst,cthd->cshd", back_weights, k_groups, preferred_element_type=jnp.float32
    )
    grad_q = grad_q.reshape(block_count, BLK, local_heads, DH)
    grad_q = grad_q + state_product("bshe,bhde->bshd", g_blocks, state_parts)
    grad_k = jnp.einsum(
        "chst,cshd->cthd", back_weights, q_groups, preferred_element_type=jnp.float32
    )
    grad_k = grad_k.reshape(block_count, BLK, local_heads, DH)
    grad_k = grad_k + state_product("bshe,bhde->bshd", v_blocks, back_parts)
    grad_v = jnp.einsum(
        "chst,cshd->cthd", attn_weights, g_groups, preferred_element_type=jnp.float32
    )
    grad_v = grad_v.reshape(block_count, BLK, local_heads, DH)
    grad_v = grad_v + state_product("bshd,bhde->bshe", k_blocks, back_parts)
    rows = queries.shape[0]
    columns = queries.shape[1]
    return (
        attended.reshape(rows, columns),
        grad_q.astype(jnp.bfloat16).reshape(rows, columns),
        grad_k.astype(jnp.bfloat16).reshape(rows, columns),
        grad_v.astype(jnp.bfloat16).reshape(rows, columns),
    )


def solution(mesh):
    tokens = P(("grp", "seq"), "head")

    def program(queries, key_rows, value_rows, grad_out, packing):
        rows = queries.shape[0] // mesh.shape["grp"] // mesh.shape["seq"]
        heads = queries.shape[1] // mesh.shape["head"] // DH
        pairs = packing.shape[0] // mesh.shape["grp"] // 3
        four = mesh.shape["seq"] == 4 and pairs == 1
        fits = rows == GROUP and heads == sum(SIZES)
        return jax.shard_map(
            exchange_body if four and fits else body,
            mesh=mesh,
            in_specs=(tokens,) * 4 + (P("grp", None),),
            out_specs=(tokens,) * 4,
            check_vma=False,
        )(queries, key_rows, value_rows, grad_out, packing)

    return program
```

```python
import functools

import jax
import jax.numpy as jnp
from jax import lax
from jax.experimental import pallas as pl
from jax.experimental.pallas import tpu as pltpu
from jax.sharding import PartitionSpec as P

DH = 128
BLK = 128
GROUP = 512
NB = GROUP // BLK
SIZES = (4, 4)
IN_SIZES = (4, 4)
ORDER = (
    ("one", 0),
    ("early", 0),
    ("one", 1),
    ("own_two", 0),
    ("two", 0),
    ("own_three", 0),
    ("in", 0),
    ("two", 1),
    ("in", 1),
    ("three", 0),
    ("base", 0),
    ("three", 1),
    ("base", 1),
    ("end", 0),
    ("end", 1),
)
MIB = 2**20
FIRST_LIMIT = 60 * MIB
SUMS_LIMIT = 12 * MIB
JOIN_LIMIT = 4 * MIB
IN_LIMIT = 16 * MIB
END_LIMIT = 16 * MIB
HELD = jnp.bfloat16
F32 = jnp.float32
BF16 = jnp.bfloat16


def flag(condition):
    return jnp.where(condition, 1, 0).astype(jnp.int32)


def either(*flags):
    out = flags[0]
    for f in flags[1:]:
        out = jnp.maximum(out, f)
    return out


def pick(index, choices):
    out = jnp.int32(0) + choices[-1]
    for n in range(len(choices) - 2, -1, -1):
        out = jnp.where(index == n, choices[n], out)
    return out


def pick_rows(index, rows):
    return [pick(index, [row[c] for row in rows]) for c in range(len(rows[0]))]


def edges(pack, blocks):
    one, two = pack[1, 0], pack[2, 0]

    def seg(b):
        return flag(b >= one) + flag(b >= two)

    first = [seg(blocks * i) for i in range(4)]
    last = [seg(blocks * i + blocks - 1) for i in range(4)]
    return seg, first, last


def message_one(pack, d, blocks):
    _, f, l = edges(pack, blocks)
    every = either(flag(l[2] == 0), flag(l[2] == 1) * flag(l[1] == 0))
    at_p, from_p = flag(l[0] == 0), flag(f[2] == 0)
    return pick_rows(
        d,
        [
            [1, 1, flag(f[2] == 1), flag(f[2] == 2)],
            [at_p, at_p, 0, 1 - at_p],
            [from_p, 0, from_p * flag(f[3] == 1), from_p * flag(f[3] == 2) + 1 - from_p],
            [0, every, either(every, flag(l[2] == 1)), either(every, flag(l[2] == 2))],
        ],
    )


def message_two(pack, d, blocks):
    _, f, l = edges(pack, blocks)
    return pick_rows(
        d,
        [
            [flag(l[0] == 0), 1, 1, 0, 0],
            [1, 1, 1, flag(f[2] == 1), flag(f[2] == 2)],
            [
                1 - flag(l[1] == 1) * flag(l[2] == 2),
                0,
                flag(l[1] == 0),
                flag(l[1] <= 1),
                flag(l[1] != 1),
            ],
            [flag(f[2] != 0), 0, 0, 0, 1],
        ],
    )


def message_three(pack, d, blocks):
    _, f, l = edges(pack, blocks)
    from_p, at_p, first_p = flag(f[2] == 0), flag(l[1] == 0), flag(f[1] == 0)
    return pick_rows(
        d,
        [
            [first_p, 1, 0, 1 - first_p, 0],
            [
                1 - flag(l[0] == 1) * flag(l[1] == 2),
                0,
                flag(l[0] == 0),
                flag(l[0] <= 1),
                flag(l[0] != 1),
            ],
            [
                either(from_p, flag(f[2] == f[3])),
                1,
                from_p,
                (1 - from_p) * flag(f[3] == 1),
                (1 - from_p) * flag(f[3] == 2),
            ],
            [1 - at_p, 0, 0, at_p, 0],
        ],
    )


def state_table(pack, d, blocks):
    _, f, l = edges(pack, blocks)
    apart = flag(f[2] == 1) * flag(l[1] != 0)
    from_p = flag(f[2] == 0)
    crossing = (1 - from_p) * flag(f[3] == 1)
    forward = [
        pick_rows(d, [[0, 0, 0], [1, 0, 0], [0, 1, 0], [0, 0, 1]]),
        pick_rows(
            d,
            [
                [0, 0, 0],
                [1, 0, flag(f[1] == 1) * flag(f[2] == 2)],
                [0, 1, 0],
                [from_p * flag(f[3] == 1), 0, 1],
            ],
        ),
        pick_rows(
            d,
            [
                [0, 0, 0],
                [1, 0, 0],
                [0, 1 - apart, apart],
                [
                    from_p * flag(f[3] == 2),
                    either(crossing, (1 - from_p) * flag(f[2] != f[3])),
                    1 - crossing,
                ],
            ],
        ),
    ]
    backward = [
        pick_rows(
            d,
            [
                [
                    flag(l[0] == 1),
                    either(flag(l[0] == 1), flag(l[0] == 0) * flag(l[1] == 1)),
                    1,
                ],
                [0, 1, flag(l[1] == 1)],
                [1, 0, 0],
                [0, 0, 0],
            ],
        ),
        pick_rows(
            d,
            [
                [0, 0, flag(l[0] == 1)],
                [0, flag(l[1] == 1), 0],
                [flag(l[2] == 1) * flag(l[1] != 0), 0, flag(l[2] == 1) * flag(l[1] == 0)],
                [0, 0, 0],
            ],
        ),
        pick_rows(
            d,
            [
                [0, 0, flag(l[0] == 2)],
                [0, flag(l[1] == 2), 0],
                [flag(l[2] == 2), 0, 0],
                [0, 0, 0],
            ],
        ),
    ]
    return forward, backward


SHORT = pl.CostEstimate(flops=1, bytes_accessed=1, transcendentals=0)
SMEM = pl.BlockSpec(memory_space=pltpu.SMEM)
ANY = pl.BlockSpec(memory_space=pl.ANY)
HBM = pl.BlockSpec(memory_space=pltpu.HBM)
VMEM = pl.BlockSpec(memory_space=pltpu.VMEM)


def order_spec(after):
    return SMEM if after.dtype == jnp.int32 else ANY


def fill_scale(pack, d, scale_ref, sign_ref):
    seg, _, _ = edges(pack, NB)
    prompt = pack[0, 1] - pack[0, 0]
    for b in range(NB):
        block = d * NB + b
        s = seg(block)
        start = pick(s, [pack[0, 0], pack[1, 0], pack[2, 0]])
        role = pick(s, [pack[0, 3], pack[1, 3], pack[2, 3]])
        base = (block - start) * BLK + 1 + jnp.where(role != 0, prompt * BLK, 0)
        seen = base + lax.broadcasted_iota(jnp.int32, (BLK, DH), 0)
        scale = lax.rsqrt((seen * DH).astype(F32))
        rows = pl.ds(b * BLK, BLK)
        if scale_ref is not None:
            scale_ref[rows, :] = scale
        sign_ref[rows, :] = jnp.where(role == 2, -1.0, 1.0) * scale


def weighted(rows, weight):
    return (rows.astype(F32) * weight).astype(BF16)


def contract_rows(a, b):
    return lax.dot_general(a, b, (((0,), (0,)), ((), ())), preferred_element_type=F32)


def contract_cols(a, b):
    return lax.dot_general(a, b, (((1,), (1,)), ((), ())), preferred_element_type=F32)


def plain(a, b):
    return lax.dot_general(a, b, (((1,), (0,)), ((), ())), preferred_element_type=F32)


def sums_kernel(messages, first, sizes, pack, place, q_hbm, k_hbm, v_hbm, g_hbm, after, *refs):
    many, chunks = len(messages), len(sizes)
    outs = refs[: many * chunks]
    left, right, total, weight_ref, sign_ref, in_sems, out_sems = refs[many * chunks :]
    d = place[0]
    seg, _, _ = edges(pack, NB)
    tables = [m(pack, d, NB)[-4:] for m in messages]
    starts = [sum(sizes[:c]) for c in range(chunks)]

    def copies(m, c, sources):
        there = pl.ds((first + starts[c]) * DH, sizes[c] * DH)
        here = pl.ds(starts[c] * DH, sizes[c] * DH)
        return [
            pltpu.make_async_copy(src.at[:, there], dst.at[m, :, here], in_sems.at[m, n, c])
            for n, (src, dst) in enumerate(zip(sources, (left, right)))
        ]

    def result(m, c):
        heads = pl.ds(starts[c], sizes[c])
        return pltpu.make_async_copy(total.at[m, heads], outs[m * chunks + c], out_sems.at[m, c])

    for m in range(many):
        for kind, sources in ((1, (k_hbm, v_hbm)), (0, (q_hbm, g_hbm))):

            @pl.when(tables[m][0] == kind)
            def _():
                for c in range(chunks):
                    for copy in copies(m, c, sources):
                        copy.start()

    fill_scale(pack, d, None, sign_ref)
    for m in range(many):
        forward = tables[m][0] == 1
        for b in range(NB):
            rows = pl.ds(b * BLK, BLK)
            takes = pick(seg(d * NB + b), tables[m][1:]).astype(F32)
            weight_ref[m, rows, :] = jnp.where(forward, 1.0, sign_ref[rows, :]) * takes
    for m in range(many):
        for c in range(chunks):
            for copy in copies(m, c, (k_hbm, v_hbm)):
                copy.wait()
            for h in range(starts[c], starts[c] + sizes[c]):
                cols = pl.ds(h * DH, DH)
                rows = weighted(right[m, :, cols], weight_ref[m])
                total[m, h] = contract_rows(left[m, :, cols], rows)
            result(m, c).start()
    for m in range(many):
        for c in range(chunks):
            result(m, c).wait()


def local_sums(messages, first, sizes, scalars, tokens, after, limit):
    rows, heads, many = tokens[0].shape[0], sum(sizes), len(messages)
    out = pl.pallas_call(
        functools.partial(sums_kernel, messages, first, sizes),
        out_shape=[
            jax.ShapeDtypeStruct((size, DH, DH), F32) for _ in messages for size in sizes
        ],
        in_specs=[SMEM, SMEM] + [HBM] * 4 + [ANY],
        out_specs=[ANY] * (many * len(sizes)),
        scratch_shapes=[
            pltpu.VMEM((many, rows, heads * DH), BF16),
            pltpu.VMEM((many, rows, heads * DH), BF16),
            pltpu.VMEM((many, heads, DH, DH), F32),
            pltpu.VMEM((many, rows, DH), F32),
            pltpu.VMEM((rows, DH), F32),
            pltpu.SemaphoreType.DMA((many, 2, len(sizes))),
            pltpu.SemaphoreType.DMA((many, len(sizes))),
        ],
        compiler_params=pltpu.CompilerParams(vmem_limit_bytes=limit),
        cost_estimate=SHORT,
        name="local_sums",
    )(*scalars, *tokens, after)
    return [out[m * len(sizes) : (m + 1) * len(sizes)] for m in range(many)]


def join_kernel(message, pack, place, got_ref, own_ref, after, out_ref):
    keep = message(pack, place[0], NB)[0] == 1

    @pl.when(keep)
    def _():
        out_ref[...] = got_ref[...] + own_ref[...]

    @pl.when(jnp.logical_not(keep))
    def _():
        out_ref[...] = own_ref[...]


def join(message, scalars, got, own, after):
    block = pl.BlockSpec(got.shape, lambda i: (0, 0, 0))
    return pl.pallas_call(
        functools.partial(join_kernel, message),
        out_shape=jax.ShapeDtypeStruct(got.shape, F32),
        grid=(1,),
        in_specs=[SMEM, SMEM, block, block, order_spec(after)],
        out_specs=block,
        compiler_params=pltpu.CompilerParams(vmem_limit_bytes=JOIN_LIMIT),
        cost_estimate=SHORT,
        name="join",
    )(*scalars, got, own, after)


def inside_kernel(per, pack, place, q_ref, k_ref, v_ref, g_ref, *refs):
    o1, o2, o3, o4, mask_ref, sign_ref = refs[-6:]
    d = place[0]
    half = GROUP // 2

    @pl.when(pl.program_id(0) == 0)
    def _():
        fill_scale(pack, d, None, sign_ref)
        seg, _, _ = edges(pack, NB)
        segs = [seg(d * NB + b) for b in range(NB)]
        tri = lax.broadcasted_iota(jnp.int32, (BLK, BLK), 0) >= lax.broadcasted_iota(
            jnp.int32, (BLK, BLK), 1
        )
        for t in range(NB):
            for s in range(NB):
                if s > t:
                    tile = jnp.zeros((BLK, BLK), F32)
                elif s == t:
                    tile = jnp.where(tri, 1.0, 0.0)
                else:
                    sees = either(flag(segs[t] == segs[s]), flag(segs[s] == 0))
                    tile = jnp.full((BLK, BLK), sees.astype(F32))
                mask_ref[pl.ds(t * BLK, BLK), pl.ds(s * BLK, BLK)] = tile.astype(BF16)

    lo, hi, whole = slice(0, half), slice(half, GROUP), slice(0, GROUP)
    for h in range(per):
        cols = slice(h * DH, (h + 1) * DH)
        q, k, v = q_ref[:, cols], k_ref[:, cols], v_ref[:, cols]
        g = weighted(g_ref[:, cols], sign_ref[...])

        def masked(a, b, rows, keys):
            return contract_cols(a[rows], b[keys]).astype(BF16) * mask_ref[rows, keys]

        def put(ref, rows, value):
            ref[rows, cols] = value.astype(ref.dtype)

        s_lo = masked(q, k, lo, lo)
        s_hi = masked(q, k, hi, whole)
        put(o1, lo, plain(s_lo, v[lo]))
        put(o1, hi, plain(s_hi, v))
        gv = contract_rows(s_hi, g[hi])
        put(o4, lo, gv[lo] + contract_rows(s_lo, g[lo]))
        put(o4, hi, gv[hi])
        b_lo = masked(g, v, lo, lo)
        b_hi = masked(g, v, hi, whole)
        put(o2, lo, plain(b_lo, k[lo]))
        put(o2, hi, plain(b_hi, k))
        gk = contract_rows(b_hi, q[hi])
        put(o3, lo, gk[lo] + contract_rows(b_lo, q[lo]))
        put(o3, hi, gk[hi])


def inside_products(first, heads, scalars, tokens, before, after):
    rows, cols = tokens[0].shape
    per = 2 if first % 2 == 0 and heads % 2 == 0 else 1
    spec = pl.BlockSpec((rows, per * DH), lambda i: (0, first // per + i))
    operands = [*scalars, *tokens, after]
    specs = [SMEM, SMEM] + [spec] * 4 + [order_spec(after)]
    aliases = {}
    if before is not None:
        aliases = {len(operands) + n: n for n in range(4)}
        operands += list(before)
        specs += [ANY] * 4
    return pl.pallas_call(
        functools.partial(inside_kernel, per),
        out_shape=[jax.ShapeDtypeStruct((rows, cols), HELD)] * 4,
        grid=(heads // per,),
        in_specs=specs,
        out_specs=[spec] * 4,
        scratch_shapes=[pltpu.VMEM((rows, rows), BF16), pltpu.VMEM((rows, DH), F32)],
        input_output_aliases=aliases,
        compiler_params=pltpu.CompilerParams(vmem_limit_bytes=IN_LIMIT),
        cost_estimate=SHORT,
        name="inside_products",
    )(*operands)


def base_kernel(first, heads, pack, place, *refs):
    q_ref, k_ref, v_ref, g_ref, i1, i2, i3, i4, r1, r2, _ = refs[:11]
    o1, o2, o3, o4, sign_ref, both_ref = refs[11:]
    d = place[0]
    fill_scale(pack, d, None, sign_ref)
    seg, _, _ = edges(pack, NB)
    segs = [seg(d * NB + b) for b in range(NB)]
    tables = state_table(pack, d, NB)
    weights = [[[w.astype(F32) for w in row] for row in table] for table in tables]
    both_ref[...] = jnp.zeros_like(both_ref)
    for h in range(heads):
        here = slice(h * DH, (h + 1) * DH)
        cols = slice((first + h) * DH, (first + h + 1) * DH)
        for x in range(3):
            for n, table in enumerate(weights):
                total = table[x][0] * r1[h] + table[x][1] * r2[h]
                part = slice(n * DH, (n + 1) * DH)
                both_ref[h, x, part, part] = total.astype(BF16)
        for b in range(NB):
            rows = slice(b * BLK, (b + 1) * BLK)
            states = both_ref[h, segs[b]]
            q, k, v = q_ref[rows, cols], k_ref[rows, cols], v_ref[rows, cols]
            g = weighted(g_ref[rows, cols], sign_ref[rows, :])
            one = plain(jnp.concatenate([q, k], axis=1), states)
            two = contract_cols(jnp.concatenate([g, v], axis=1), states)
            o1[rows, here] = i1[rows, cols].astype(F32) + one[:, :DH]
            o4[rows, here] = i4[rows, cols].astype(F32) + one[:, DH:]
            o2[rows, here] = i2[rows, cols].astype(F32) + two[:, :DH]
            o3[rows, here] = i3[rows, cols].astype(F32) + two[:, DH:]


def base_products(first, heads, scalars, tokens, inside, got, after):
    rows = tokens[0].shape[0]
    return pl.pallas_call(
        functools.partial(base_kernel, first, heads),
        out_shape=[jax.ShapeDtypeStruct((rows, heads * DH), F32)] * 4,
        in_specs=[SMEM, SMEM] + [VMEM] * 10 + [order_spec(after)],
        out_specs=[VMEM] * 4,
        scratch_shapes=[
            pltpu.VMEM((rows, DH), F32),
            pltpu.VMEM((heads, 3, 2 * DH, 2 * DH), BF16),
        ],
        compiler_params=pltpu.CompilerParams(vmem_limit_bytes=END_LIMIT),
        cost_estimate=SHORT,
        name="base_products",
    )(*scalars, *tokens, *inside, *got, after)


def final_kernel(first, heads, pack, place, *refs):
    q_ref, k_ref, v_ref, g_ref, i1, i2, i3, i4, r3 = refs[:9]
    outs = refs[-12:-8]
    b1, b2, b3, b4, scale_ref, sign_ref, both_ref, sems = refs[-8:]
    d = place[0]
    fill_scale(pack, d, scale_ref, sign_ref)
    seg, _, _ = edges(pack, NB)
    segs = [seg(d * NB + b) for b in range(NB)]
    ahead, behind = [
        [pick(s, [row[2] for row in table]).astype(F32) for s in segs]
        for table in state_table(pack, d, NB)
    ]
    both_ref[...] = jnp.zeros_like(both_ref)
    held = ((b1, outs[0]), (b2, outs[1]), (b3, outs[2]), (b4, outs[3]))

    def copies(h):
        return [
            pltpu.make_async_copy(
                buffer.at[:, pl.ds(h * DH, DH)], out.at[:, pl.ds((first + h) * DH, DH)], sems.at[n, h]
            )
            for n, (buffer, out) in enumerate(held)
        ]

    for h in range(heads):
        here = slice(h * DH, (h + 1) * DH)
        cols = slice((first + h) * DH, (first + h + 1) * DH)
        state = r3[h].astype(BF16)
        both_ref[h, :DH, :DH] = state
        both_ref[h, DH:, DH:] = state
        states = both_ref[h]
        q, k, v = q_ref[:, cols], k_ref[:, cols], v_ref[:, cols]
        g = weighted(g_ref[:, cols], sign_ref[...])
        one = plain(jnp.concatenate([q, k], axis=1), states)
        two = contract_cols(jnp.concatenate([g, v], axis=1), states)
        for b in range(NB):
            rows = slice(b * BLK, (b + 1) * BLK)
            total = i1[rows, here] + ahead[b] * one[rows, :DH]
            b1[rows, here] = (scale_ref[rows, :] * total).astype(BF16)
            b4[rows, here] = (i4[rows, here] + behind[b] * one[rows, DH:]).astype(BF16)
            b2[rows, here] = (i2[rows, here] + ahead[b] * two[rows, :DH]).astype(BF16)
            b3[rows, here] = (i3[rows, here] + behind[b] * two[rows, DH:]).astype(BF16)
        for copy in copies(h):
            copy.start()
    for h in range(heads):
        for copy in copies(h):
            copy.wait()


def final_products(first, heads, scalars, tokens, base, got, before):
    rows, cols = tokens[0].shape
    operands = [*scalars, *tokens, *base, got]
    specs = [SMEM, SMEM] + [VMEM] * 9
    aliases = {}
    if before is not None:
        aliases = {len(operands) + n: n for n in range(4)}
        operands += list(before)
        specs += [ANY] * 4
    return pl.pallas_call(
        functools.partial(final_kernel, first, heads),
        out_shape=[jax.ShapeDtypeStruct((rows, cols), BF16)] * 4,
        in_specs=specs,
        out_specs=[ANY] * 4,
        scratch_shapes=[pltpu.VMEM((rows, heads * DH), BF16)] * 4
        + [
            pltpu.VMEM((rows, DH), F32),
            pltpu.VMEM((rows, DH), F32),
            pltpu.VMEM((heads, 2 * DH, 2 * DH), BF16),
            pltpu.SemaphoreType.DMA((4, heads)),
        ],
        input_output_aliases=aliases,
        compiler_params=pltpu.CompilerParams(vmem_limit_bytes=END_LIMIT),
        cost_estimate=SHORT,
        name="final_products",
    )(*operands)


def exchange_body(queries, key_rows, value_rows, grad_out, packing):
    place = lax.axis_index("seq").astype(jnp.int32).reshape(1)
    scalars = (packing, place)
    tokens = (queries, key_rows, value_rows, grad_out)
    starts = [sum(SIZES[:c]) for c in range(len(SIZES))]
    near = [(i, i ^ 1) for i in range(4)]
    across = [(i, 3 - i) for i in range(4)]

    count = len(SIZES)
    one, two, three = [None] * count, [None] * count, [None] * count
    early = local_sums((message_one,), 0, SIZES[:1], scalars, tokens, packing, FIRST_LIMIT)[0]
    last = early[0]
    inside, out, base = None, None, [None] * count
    for what, c in ORDER:
        if what == "one":
            one[c] = lax.ppermute(early[c], "seq", near)
        elif what == "early":
            early += local_sums(
                (message_one,), SIZES[0], SIZES[1:], scalars, tokens, last, SUMS_LIMIT
            )[0]
            last = early[-1]
        elif what == "own_two":
            (own_two,) = local_sums((message_two,), 0, SIZES, scalars, tokens, last, SUMS_LIMIT)
            last = own_two[0]
        elif what == "own_three":
            (own_three,) = local_sums(
                (message_three,), 0, SIZES, scalars, tokens, last, SUMS_LIMIT
            )
            last = own_three[0]
        elif what == "base":
            got = (one[c], two[c])
            base[c] = base_products(starts[c], SIZES[c], scalars, tokens, inside, got, last)
            last = base[c][0]
        elif what == "two":
            last = join(message_two, scalars, one[c], own_two[c], last)
            two[c] = lax.ppermute(last, "seq", across)
        elif what == "three":
            last = join(message_three, scalars, two[c], own_three[c], last)
            three[c] = lax.ppermute(last, "seq", near)
        elif what == "in":
            first = 0 if inside is None else sum(IN_SIZES[:c])
            inside = inside_products(first, IN_SIZES[c], scalars, tokens, inside, last)
            last = inside[0]
        else:
            out = final_products(starts[c], SIZES[c], scalars, tokens, base[c], three[c], out)
            last = out[0]
    return tuple(out)


highest = lax.Precision.HIGHEST


def carried_in(value, axis, combine, identity, reverse):
    length, index = (lax.axis_size(axis), lax.axis_index(axis))
    everything = jax.tree.map(lambda part: lax.all_gather(part, axis), value)
    start = jax.tree.map(
        lambda part, zero: jnp.broadcast_to(jnp.asarray(zero, part.dtype), part.shape),
        value,
        identity,
    )

    def turn(k, before):
        at = length - 1 - k if reverse else k
        reached = at > index if reverse else at < index
        new = combine(before, jax.tree.map(lambda part: part[at], everything))
        return jax.tree.map(lambda a, b: jnp.where(reached, a, b), new, before)

    return lax.fori_loop(0, length, turn, start)


def block_info(packing, first_block, block_count):
    seg_starts = packing[:, 0]
    seg_ends = packing[:, 1]
    pair_col = packing[:, 2]
    role_col = packing[:, 3]
    blocks = first_block + jnp.arange(block_count, dtype=jnp.int32)
    segment = jnp.sum((seg_starts[None, :] <= blocks[:, None]).astype(jnp.int32), axis=1) - 1
    seg_ranks = jnp.arange(seg_starts.shape[0], dtype=jnp.int32)
    select = segment[:, None] == seg_ranks[None, :]
    block_role = jnp.sum(jnp.where(select, role_col[None, :], 0), axis=1)
    block_pair = jnp.sum(jnp.where(select, pair_col[None, :], 0), axis=1)
    opening = jnp.sum(jnp.where(select, seg_starts[None, :], 0), axis=1)
    prompt_sel = (segment // 3 * 3)[:, None] == seg_ranks[None, :]
    prompt_len = jnp.sum(jnp.where(prompt_sel, (seg_ends - seg_starts)[None, :], 0), axis=1)
    position = (blocks - opening)[:, None] * BLK + jnp.arange(BLK, dtype=jnp.int32)[None, :]
    visible = position + 1 + jnp.where(block_role != 0, prompt_len * BLK, 0)[:, None]
    tok_scale = lax.rsqrt((visible * DH).astype(jnp.float32))
    return (segment, block_role, block_pair, tok_scale)


def link_combine(before, behind):
    back_a, open_a, state_a = before
    back_b, open_b, state_b = behind
    empty_b = open_b < 0.0
    joins = (back_b == open_b) & (open_a == back_b) | empty_b
    state = state_b + jnp.where(joins, state_a, jnp.zeros_like(state_a))
    back_id = jnp.where(open_a < 0.0, back_b, back_a)
    open_id = jnp.where(empty_b, open_a, open_b)
    return (back_id, open_id, state)


def pick_state(carry_open, carry_state, block_ids, allowed):
    chosen = (carry_open == block_ids.astype(jnp.float32)) & allowed
    return jnp.where(chosen[:, None, None, None], carry_state[None], 0.0)


def masked_sum(flags, states):
    return jnp.einsum("j,jhde->hde", flags.astype(jnp.float32), states, precision=highest)


def split_state(state):
    upper = state.astype(jnp.bfloat16)
    upper_wide = lax.optimization_barrier(upper).astype(jnp.float32)
    lower = (state - upper_wide).astype(jnp.bfloat16)
    return (upper, lower)


def state_product(form, token_rows, parts):
    first = jnp.einsum(form, token_rows, parts[0], preferred_element_type=jnp.float32)
    return first + jnp.einsum(form, token_rows, parts[1], preferred_element_type=jnp.float32)


def body(queries, key_rows, value_rows, grad_out, packing):
    block_count = queries.shape[0] // BLK
    local_heads = queries.shape[1] // DH
    group_count = queries.shape[0] // GROUP
    final_index = block_count - 1
    first_block = lax.axis_index("seq") * block_count
    segment, block_role, block_pair, tok_scale = block_info(packing, first_block, block_count)
    dpo_sign = jnp.where(block_role == 2, -1.0, 1.0).astype(jnp.float32)
    q_blocks = queries.reshape(block_count, BLK, local_heads, DH)
    k_blocks = key_rows.reshape(block_count, BLK, local_heads, DH)
    v_blocks = value_rows.reshape(block_count, BLK, local_heads, DH)
    weight = (dpo_sign[:, None] * tok_scale)[:, :, None, None]
    g_blocks = (
        weight * grad_out.reshape(block_count, BLK, local_heads, DH).astype(jnp.float32)
    ).astype(jnp.bfloat16)
    block_kv = jnp.einsum("bshd,bshe->bhde", k_blocks, v_blocks, preferred_element_type=jnp.float32)
    block_qg = jnp.einsum("bshd,bshe->bhde", q_blocks, g_blocks, preferred_element_type=jnp.float32)
    group_of = jnp.arange(block_count, dtype=jnp.int32) // (GROUP // BLK)
    same_seg = segment[:, None] == segment[None, :]
    link = same_seg & (group_of[None, :] < group_of[:, None])
    seg_first = segment[0].astype(jnp.float32)
    seg_last = segment[final_index].astype(jnp.float32)
    neutral = jnp.full((), -1.0, jnp.float32)
    zero_state = jnp.zeros((local_heads, DH, DH), jnp.float32)
    is_prompt = block_role == 0
    is_reply = block_role != 0
    pair_count = packing.shape[0] // 3
    pair_hot = (block_pair[:, None] == jnp.arange(pair_count, dtype=jnp.int32)[None, :]).astype(
        jnp.float32
    )
    fwd_seg = masked_sum(segment == segment[final_index], block_kv)
    carried = carried_in(
        (seg_first, seg_last, fwd_seg), "seq", link_combine, (neutral, neutral, zero_state), False
    )
    prompt_part = jnp.einsum(
        "jp,jhde->phde",
        pair_hot * is_prompt[:, None].astype(jnp.float32),
        block_kv,
        precision=highest,
    )
    prompt_all = lax.psum(prompt_part, "seq")
    outside_in = pick_state(carried[1], carried[2], segment, is_reply | is_prompt)
    outside_in = outside_in + jnp.einsum(
        "bp,phde->bhde",
        pair_hot * is_reply[:, None].astype(jnp.float32),
        prompt_all,
        precision=highest,
    )
    rev_seg = masked_sum(segment == segment[0], block_qg)
    returned = carried_in(
        (seg_last, seg_first, rev_seg), "seq", link_combine, (neutral, neutral, zero_state), True
    )
    reply_part = jnp.einsum(
        "jp,jhde->phde",
        pair_hot * is_reply[:, None].astype(jnp.float32),
        block_qg,
        precision=highest,
    )
    reply_all = lax.psum(reply_part, "seq")
    outside_back = pick_state(returned[1], returned[2], segment, is_reply | is_prompt)
    outside_back = outside_back + jnp.einsum(
        "bp,phde->bhde",
        pair_hot * is_prompt[:, None].astype(jnp.float32),
        reply_all,
        precision=highest,
    )
    link_f = link.astype(jnp.float32)
    state = jnp.einsum("bj,jhde->bhde", link_f, block_kv, precision=highest) + outside_in
    back_state = jnp.einsum("bj,bhde->jhde", link_f, block_qg, precision=highest) + outside_back
    state_parts = split_state(state)
    back_parts = split_state(back_state)
    tok_seg = jnp.repeat(segment, BLK).reshape(group_count, GROUP)
    places = jnp.arange(GROUP, dtype=jnp.int32)
    causal = (tok_seg[:, :, None] == tok_seg[:, None, :]) & (
        places[None, :, None] >= places[None, None, :]
    )
    q_groups = queries.reshape(group_count, GROUP, local_heads, DH)
    k_groups = key_rows.reshape(group_count, GROUP, local_heads, DH)
    v_groups = value_rows.reshape(group_count, GROUP, local_heads, DH)
    g_groups = g_blocks.reshape(group_count, GROUP, local_heads, DH)
    scores = jnp.einsum("cshd,cthd->chst", q_groups, k_groups, preferred_element_type=jnp.float32)
    attn_weights = jnp.where(causal[:, None], scores, 0.0).astype(jnp.bfloat16)
    inside = jnp.einsum(
        "chst,cthd->cshd", attn_weights, v_groups, preferred_element_type=jnp.float32
    )
    inside = inside.reshape(block_count, BLK, local_heads, DH)
    outside = state_product("bshd,bhde->bshe", q_blocks, state_parts)
    attended = (tok_scale[:, :, None, None] * (inside + outside)).astype(jnp.bfloat16)
    back_raw = jnp.einsum("cshd,cthd->chst", g_groups, v_groups, preferred_element_type=jnp.float32)
    back_weights = jnp.where(causal[:, None], back_raw, 0.0).astype(jnp.bfloat16)
    grad_q = jnp.einsum(
        "chst,cthd->cshd", back_weights, k_groups, preferred_element_type=jnp.float32
    )
    grad_q = grad_q.reshape(block_count, BLK, local_heads, DH)
    grad_q = grad_q + state_product("bshe,bhde->bshd", g_blocks, state_parts)
    grad_k = jnp.einsum(
        "chst,cshd->cthd", back_weights, q_groups, preferred_element_type=jnp.float32
    )
    grad_k = grad_k.reshape(block_count, BLK, local_heads, DH)
    grad_k = grad_k + state_product("bshe,bhde->bshd", v_blocks, back_parts)
    grad_v = jnp.einsum(
        "chst,cshd->cthd", attn_weights, g_groups, preferred_element_type=jnp.float32
    )
    grad_v = grad_v.reshape(block_count, BLK, local_heads, DH)
    grad_v = grad_v + state_product("bshd,bhde->bshe", k_blocks, back_parts)
    rows = queries.shape[0]
    columns = queries.shape[1]
    return (
        attended.reshape(rows, columns),
        grad_q.astype(jnp.bfloat16).reshape(rows, columns),
        grad_k.astype(jnp.bfloat16).reshape(rows, columns),
        grad_v.astype(jnp.bfloat16).reshape(rows, columns),
    )


def solution(mesh):
    tokens = P(("grp", "seq"), "head")

    def program(queries, key_rows, value_rows, grad_out, packing):
        rows = queries.shape[0] // mesh.shape["grp"] // mesh.shape["seq"]
        heads = queries.shape[1] // mesh.shape["head"] // DH
        pairs = packing.shape[0] // mesh.shape["grp"] // 3
        four = mesh.shape["seq"] == 4 and pairs == 1
        fits = rows == GROUP and heads == sum(SIZES)
        return jax.shard_map(
            exchange_body if four and fits else body,
            mesh=mesh,
            in_specs=(tokens,) * 4 + (P("grp", None),),
            out_specs=(tokens,) * 4,
            check_vma=False,
        )(queries, key_rows, value_rows, grad_out, packing)

    return program
```

```python
import functools

import jax
import jax.numpy as jnp
from jax import lax
from jax.experimental import pallas as pl
from jax.experimental.pallas import tpu as pltpu
from jax.sharding import PartitionSpec as P

DH = 128
BLK = 128
GROUP = 512
NB = GROUP // BLK
SIZES = (4, 4)
IN_SIZES = (4, 4)
ORDER = (
    ("one", 0),
    ("early", 0),
    ("one", 1),
    ("own_two", 0),
    ("two", 0),
    ("in", 0),
    ("two", 1),
    ("own_three", 0),
    ("in", 1),
    ("three", 0),
    ("base", 0),
    ("three", 1),
    ("base", 1),
    ("end", 0),
    ("end", 1),
)
MIB = 2**20
FIRST_LIMIT = 60 * MIB
SUMS_LIMIT = 12 * MIB
JOIN_LIMIT = 4 * MIB
IN_LIMIT = 16 * MIB
END_LIMIT = 16 * MIB
HELD = jnp.bfloat16
F32 = jnp.float32
BF16 = jnp.bfloat16


def flag(condition):
    return jnp.where(condition, 1, 0).astype(jnp.int32)


def either(*flags):
    out = flags[0]
    for f in flags[1:]:
        out = jnp.maximum(out, f)
    return out


def pick(index, choices):
    out = jnp.int32(0) + choices[-1]
    for n in range(len(choices) - 2, -1, -1):
        out = jnp.where(index == n, choices[n], out)
    return out


def pick_rows(index, rows):
    return [pick(index, [row[c] for row in rows]) for c in range(len(rows[0]))]


def edges(pack, blocks):
    one, two = pack[1, 0], pack[2, 0]

    def seg(b):
        return flag(b >= one) + flag(b >= two)

    first = [seg(blocks * i) for i in range(4)]
    last = [seg(blocks * i + blocks - 1) for i in range(4)]
    return seg, first, last


def message_one(pack, d, blocks):
    _, f, l = edges(pack, blocks)
    every = either(flag(l[2] == 0), flag(l[2] == 1) * flag(l[1] == 0))
    at_p, from_p = flag(l[0] == 0), flag(f[2] == 0)
    return pick_rows(
        d,
        [
            [1, 1, flag(f[2] == 1), flag(f[2] == 2)],
            [at_p, at_p, 0, 1 - at_p],
            [from_p, 0, from_p * flag(f[3] == 1), from_p * flag(f[3] == 2) + 1 - from_p],
            [0, every, either(every, flag(l[2] == 1)), either(every, flag(l[2] == 2))],
        ],
    )


def message_two(pack, d, blocks):
    _, f, l = edges(pack, blocks)
    return pick_rows(
        d,
        [
            [flag(l[0] == 0), 1, 1, 0, 0],
            [1, 1, 1, flag(f[2] == 1), flag(f[2] == 2)],
            [
                1 - flag(l[1] == 1) * flag(l[2] == 2),
                0,
                flag(l[1] == 0),
                flag(l[1] <= 1),
                flag(l[1] != 1),
            ],
            [flag(f[2] != 0), 0, 0, 0, 1],
        ],
    )


def message_three(pack, d, blocks):
    _, f, l = edges(pack, blocks)
    from_p, at_p, first_p = flag(f[2] == 0), flag(l[1] == 0), flag(f[1] == 0)
    return pick_rows(
        d,
        [
            [first_p, 1, 0, 1 - first_p, 0],
            [
                1 - flag(l[0] == 1) * flag(l[1] == 2),
                0,
                flag(l[0] == 0),
                flag(l[0] <= 1),
                flag(l[0] != 1),
            ],
            [
                either(from_p, flag(f[2] == f[3])),
                1,
                from_p,
                (1 - from_p) * flag(f[3] == 1),
                (1 - from_p) * flag(f[3] == 2),
            ],
            [1 - at_p, 0, 0, at_p, 0],
        ],
    )


def state_table(pack, d, blocks):
    _, f, l = edges(pack, blocks)
    apart = flag(f[2] == 1) * flag(l[1] != 0)
    from_p = flag(f[2] == 0)
    crossing = (1 - from_p) * flag(f[3] == 1)
    forward = [
        pick_rows(d, [[0, 0, 0], [1, 0, 0], [0, 1, 0], [0, 0, 1]]),
        pick_rows(
            d,
            [
                [0, 0, 0],
                [1, 0, flag(f[1] == 1) * flag(f[2] == 2)],
                [0, 1, 0],
                [from_p * flag(f[3] == 1), 0, 1],
            ],
        ),
        pick_rows(
            d,
            [
                [0, 0, 0],
                [1, 0, 0],
                [0, 1 - apart, apart],
                [
                    from_p * flag(f[3] == 2),
                    either(crossing, (1 - from_p) * flag(f[2] != f[3])),
                    1 - crossing,
                ],
            ],
        ),
    ]
    backward = [
        pick_rows(
            d,
            [
                [
                    flag(l[0] == 1),
                    either(flag(l[0] == 1), flag(l[0] == 0) * flag(l[1] == 1)),
                    1,
                ],
                [0, 1, flag(l[1] == 1)],
                [1, 0, 0],
                [0, 0, 0],
            ],
        ),
        pick_rows(
            d,
            [
                [0, 0, flag(l[0] == 1)],
                [0, flag(l[1] == 1), 0],
                [flag(l[2] == 1) * flag(l[1] != 0), 0, flag(l[2] == 1) * flag(l[1] == 0)],
                [0, 0, 0],
            ],
        ),
        pick_rows(
            d,
            [
                [0, 0, flag(l[0] == 2)],
                [0, flag(l[1] == 2), 0],
                [flag(l[2] == 2), 0, 0],
                [0, 0, 0],
            ],
        ),
    ]
    return forward, backward


SHORT = pl.CostEstimate(flops=1, bytes_accessed=1, transcendentals=0)
SMEM = pl.BlockSpec(memory_space=pltpu.SMEM)
ANY = pl.BlockSpec(memory_space=pl.ANY)
HBM = pl.BlockSpec(memory_space=pltpu.HBM)
VMEM = pl.BlockSpec(memory_space=pltpu.VMEM)


def order_spec(after):
    return SMEM if after.dtype == jnp.int32 else ANY


def fill_scale(pack, d, scale_ref, sign_ref):
    seg, _, _ = edges(pack, NB)
    prompt = pack[0, 1] - pack[0, 0]
    for b in range(NB):
        block = d * NB + b
        s = seg(block)
        start = pick(s, [pack[0, 0], pack[1, 0], pack[2, 0]])
        role = pick(s, [pack[0, 3], pack[1, 3], pack[2, 3]])
        base = (block - start) * BLK + 1 + jnp.where(role != 0, prompt * BLK, 0)
        seen = base + lax.broadcasted_iota(jnp.int32, (BLK, DH), 0)
        scale = lax.rsqrt((seen * DH).astype(F32))
        rows = pl.ds(b * BLK, BLK)
        if scale_ref is not None:
            scale_ref[rows, :] = scale
        sign_ref[rows, :] = jnp.where(role == 2, -1.0, 1.0) * scale


def weighted(rows, weight):
    return (rows.astype(F32) * weight).astype(BF16)


def contract_rows(a, b):
    return lax.dot_general(a, b, (((0,), (0,)), ((), ())), preferred_element_type=F32)


def contract_cols(a, b):
    return lax.dot_general(a, b, (((1,), (1,)), ((), ())), preferred_element_type=F32)


def plain(a, b):
    return lax.dot_general(a, b, (((1,), (0,)), ((), ())), preferred_element_type=F32)


def sums_kernel(messages, first, sizes, pack, place, q_hbm, k_hbm, v_hbm, g_hbm, after, *refs):
    many, chunks = len(messages), len(sizes)
    outs = refs[: many * chunks]
    left, right, total, weight_ref, sign_ref, in_sems, out_sems = refs[many * chunks :]
    d = place[0]
    seg, _, _ = edges(pack, NB)
    tables = [m(pack, d, NB)[-4:] for m in messages]
    starts = [sum(sizes[:c]) for c in range(chunks)]

    def copies(m, c, sources):
        there = pl.ds((first + starts[c]) * DH, sizes[c] * DH)
        here = pl.ds(starts[c] * DH, sizes[c] * DH)
        return [
            pltpu.make_async_copy(src.at[:, there], dst.at[m, :, here], in_sems.at[m, n, c])
            for n, (src, dst) in enumerate(zip(sources, (left, right)))
        ]

    def result(m, c):
        heads = pl.ds(starts[c], sizes[c])
        return pltpu.make_async_copy(total.at[m, heads], outs[m * chunks + c], out_sems.at[m, c])

    for m in range(many):
        for kind, sources in ((1, (k_hbm, v_hbm)), (0, (q_hbm, g_hbm))):

            @pl.when(tables[m][0] == kind)
            def _():
                for c in range(chunks):
                    for copy in copies(m, c, sources):
                        copy.start()

    fill_scale(pack, d, None, sign_ref)
    for m in range(many):
        forward = tables[m][0] == 1
        for b in range(NB):
            rows = pl.ds(b * BLK, BLK)
            takes = pick(seg(d * NB + b), tables[m][1:]).astype(F32)
            weight_ref[m, rows, :] = jnp.where(forward, 1.0, sign_ref[rows, :]) * takes
    for m in range(many):
        for c in range(chunks):
            for copy in copies(m, c, (k_hbm, v_hbm)):
                copy.wait()
            for h in range(starts[c], starts[c] + sizes[c]):
                cols = pl.ds(h * DH, DH)
                rows = weighted(right[m, :, cols], weight_ref[m])
                total[m, h] = contract_rows(left[m, :, cols], rows)
            result(m, c).start()
    for m in range(many):
        for c in range(chunks):
            result(m, c).wait()


def local_sums(messages, first, sizes, scalars, tokens, after, limit):
    rows, heads, many = tokens[0].shape[0], sum(sizes), len(messages)
    out = pl.pallas_call(
        functools.partial(sums_kernel, messages, first, sizes),
        out_shape=[
            jax.ShapeDtypeStruct((size, DH, DH), F32) for _ in messages for size in sizes
        ],
        in_specs=[SMEM, SMEM] + [HBM] * 4 + [ANY],
        out_specs=[ANY] * (many * len(sizes)),
        scratch_shapes=[
            pltpu.VMEM((many, rows, heads * DH), BF16),
            pltpu.VMEM((many, rows, heads * DH), BF16),
            pltpu.VMEM((many, heads, DH, DH), F32),
            pltpu.VMEM((many, rows, DH), F32),
            pltpu.VMEM((rows, DH), F32),
            pltpu.SemaphoreType.DMA((many, 2, len(sizes))),
            pltpu.SemaphoreType.DMA((many, len(sizes))),
        ],
        compiler_params=pltpu.CompilerParams(vmem_limit_bytes=limit),
        cost_estimate=SHORT,
        name="local_sums",
    )(*scalars, *tokens, after)
    return [out[m * len(sizes) : (m + 1) * len(sizes)] for m in range(many)]


def join_kernel(message, pack, place, got_ref, own_ref, after, out_ref):
    keep = message(pack, place[0], NB)[0] == 1

    @pl.when(keep)
    def _():
        out_ref[...] = got_ref[...] + own_ref[...]

    @pl.when(jnp.logical_not(keep))
    def _():
        out_ref[...] = own_ref[...]


def join(message, scalars, got, own, after):
    block = pl.BlockSpec(got.shape, lambda i: (0, 0, 0))
    return pl.pallas_call(
        functools.partial(join_kernel, message),
        out_shape=jax.ShapeDtypeStruct(got.shape, F32),
        grid=(1,),
        in_specs=[SMEM, SMEM, block, block, order_spec(after)],
        out_specs=block,
        compiler_params=pltpu.CompilerParams(vmem_limit_bytes=JOIN_LIMIT),
        cost_estimate=SHORT,
        name="join",
    )(*scalars, got, own, after)


def inside_kernel(per, pack, place, q_ref, k_ref, v_ref, g_ref, *refs):
    o1, o2, o3, o4, mask_ref, sign_ref = refs[-6:]
    d = place[0]
    half = GROUP // 2

    @pl.when(pl.program_id(0) == 0)
    def _():
        fill_scale(pack, d, None, sign_ref)
        seg, _, _ = edges(pack, NB)
        segs = [seg(d * NB + b) for b in range(NB)]
        tri = lax.broadcasted_iota(jnp.int32, (BLK, BLK), 0) >= lax.broadcasted_iota(
            jnp.int32, (BLK, BLK), 1
        )
        for t in range(NB):
            for s in range(NB):
                if s > t:
                    tile = jnp.zeros((BLK, BLK), F32)
                elif s == t:
                    tile = jnp.where(tri, 1.0, 0.0)
                else:
                    sees = either(flag(segs[t] == segs[s]), flag(segs[s] == 0))
                    tile = jnp.full((BLK, BLK), sees.astype(F32))
                mask_ref[pl.ds(t * BLK, BLK), pl.ds(s * BLK, BLK)] = tile.astype(BF16)

    lo, hi, whole = slice(0, half), slice(half, GROUP), slice(0, GROUP)
    for h in range(per):
        cols = slice(h * DH, (h + 1) * DH)
        q, k, v = q_ref[:, cols], k_ref[:, cols], v_ref[:, cols]
        g = weighted(g_ref[:, cols], sign_ref[...])

        def masked(a, b, rows, keys):
            return contract_cols(a[rows], b[keys]).astype(BF16) * mask_ref[rows, keys]

        def put(ref, rows, value):
            ref[rows, cols] = value.astype(ref.dtype)

        s_lo = masked(q, k, lo, lo)
        s_hi = masked(q, k, hi, whole)
        put(o1, lo, plain(s_lo, v[lo]))
        put(o1, hi, plain(s_hi, v))
        gv = contract_rows(s_hi, g[hi])
        put(o4, lo, gv[lo] + contract_rows(s_lo, g[lo]))
        put(o4, hi, gv[hi])
        b_lo = masked(g, v, lo, lo)
        b_hi = masked(g, v, hi, whole)
        put(o2, lo, plain(b_lo, k[lo]))
        put(o2, hi, plain(b_hi, k))
        gk = contract_rows(b_hi, q[hi])
        put(o3, lo, gk[lo] + contract_rows(b_lo, q[lo]))
        put(o3, hi, gk[hi])


def inside_products(first, heads, scalars, tokens, before, after):
    rows, cols = tokens[0].shape
    per = 2 if first % 2 == 0 and heads % 2 == 0 else 1
    spec = pl.BlockSpec((rows, per * DH), lambda i: (0, first // per + i))
    operands = [*scalars, *tokens, after]
    specs = [SMEM, SMEM] + [spec] * 4 + [order_spec(after)]
    aliases = {}
    if before is not None:
        aliases = {len(operands) + n: n for n in range(4)}
        operands += list(before)
        specs += [ANY] * 4
    return pl.pallas_call(
        functools.partial(inside_kernel, per),
        out_shape=[jax.ShapeDtypeStruct((rows, cols), HELD)] * 4,
        grid=(heads // per,),
        in_specs=specs,
        out_specs=[spec] * 4,
        scratch_shapes=[pltpu.VMEM((rows, rows), BF16), pltpu.VMEM((rows, DH), F32)],
        input_output_aliases=aliases,
        compiler_params=pltpu.CompilerParams(vmem_limit_bytes=IN_LIMIT),
        cost_estimate=SHORT,
        name="inside_products",
    )(*operands)


def base_kernel(first, heads, pack, place, *refs):
    q_ref, k_ref, v_ref, g_ref, i1, i2, i3, i4, r1, r2, _ = refs[:11]
    o1, o2, o3, o4, sign_ref, both_ref = refs[11:]
    d = place[0]
    fill_scale(pack, d, None, sign_ref)
    seg, _, _ = edges(pack, NB)
    segs = [seg(d * NB + b) for b in range(NB)]
    tables = state_table(pack, d, NB)
    weights = [[[w.astype(F32) for w in row] for row in table] for table in tables]
    both_ref[...] = jnp.zeros_like(both_ref)
    for h in range(heads):
        here = slice(h * DH, (h + 1) * DH)
        cols = slice((first + h) * DH, (first + h + 1) * DH)
        for x in range(3):
            for n, table in enumerate(weights):
                total = table[x][0] * r1[h] + table[x][1] * r2[h]
                part = slice(n * DH, (n + 1) * DH)
                both_ref[h, x, part, part] = total.astype(BF16)
        for b in range(NB):
            rows = slice(b * BLK, (b + 1) * BLK)
            states = both_ref[h, segs[b]]
            q, k, v = q_ref[rows, cols], k_ref[rows, cols], v_ref[rows, cols]
            g = weighted(g_ref[rows, cols], sign_ref[rows, :])
            one = plain(jnp.concatenate([q, k], axis=1), states)
            two = contract_cols(jnp.concatenate([g, v], axis=1), states)
            o1[rows, here] = i1[rows, cols].astype(F32) + one[:, :DH]
            o4[rows, here] = i4[rows, cols].astype(F32) + one[:, DH:]
            o2[rows, here] = i2[rows, cols].astype(F32) + two[:, :DH]
            o3[rows, here] = i3[rows, cols].astype(F32) + two[:, DH:]


def base_products(first, heads, scalars, tokens, inside, got, after):
    rows = tokens[0].shape[0]
    return pl.pallas_call(
        functools.partial(base_kernel, first, heads),
        out_shape=[jax.ShapeDtypeStruct((rows, heads * DH), F32)] * 4,
        in_specs=[SMEM, SMEM] + [VMEM] * 10 + [order_spec(after)],
        out_specs=[VMEM] * 4,
        scratch_shapes=[
            pltpu.VMEM((rows, DH), F32),
            pltpu.VMEM((heads, 3, 2 * DH, 2 * DH), BF16),
        ],
        compiler_params=pltpu.CompilerParams(vmem_limit_bytes=END_LIMIT),
        cost_estimate=SHORT,
        name="base_products",
    )(*scalars, *tokens, *inside, *got, after)


def final_kernel(first, heads, pack, place, *refs):
    q_ref, k_ref, v_ref, g_ref, i1, i2, i3, i4, r3 = refs[:9]
    outs = refs[-12:-8]
    b1, b2, b3, b4, scale_ref, sign_ref, both_ref, sems = refs[-8:]
    d = place[0]
    fill_scale(pack, d, scale_ref, sign_ref)
    seg, _, _ = edges(pack, NB)
    segs = [seg(d * NB + b) for b in range(NB)]
    ahead, behind = [
        [pick(s, [row[2] for row in table]).astype(F32) for s in segs]
        for table in state_table(pack, d, NB)
    ]
    both_ref[...] = jnp.zeros_like(both_ref)
    held = ((b1, outs[0]), (b2, outs[1]), (b3, outs[2]), (b4, outs[3]))

    def copies(h):
        return [
            pltpu.make_async_copy(
                buffer.at[:, pl.ds(h * DH, DH)], out.at[:, pl.ds((first + h) * DH, DH)], sems.at[n, h]
            )
            for n, (buffer, out) in enumerate(held)
        ]

    for h in range(heads):
        here = slice(h * DH, (h + 1) * DH)
        cols = slice((first + h) * DH, (first + h + 1) * DH)
        state = r3[h].astype(BF16)
        both_ref[h, :DH, :DH] = state
        both_ref[h, DH:, DH:] = state
        states = both_ref[h]
        q, k, v = q_ref[:, cols], k_ref[:, cols], v_ref[:, cols]
        g = weighted(g_ref[:, cols], sign_ref[...])
        one = plain(jnp.concatenate([q, k], axis=1), states)
        two = contract_cols(jnp.concatenate([g, v], axis=1), states)
        for b in range(NB):
            rows = slice(b * BLK, (b + 1) * BLK)
            total = i1[rows, here] + ahead[b] * one[rows, :DH]
            b1[rows, here] = (scale_ref[rows, :] * total).astype(BF16)
            b4[rows, here] = (i4[rows, here] + behind[b] * one[rows, DH:]).astype(BF16)
            b2[rows, here] = (i2[rows, here] + ahead[b] * two[rows, :DH]).astype(BF16)
            b3[rows, here] = (i3[rows, here] + behind[b] * two[rows, DH:]).astype(BF16)
        for copy in copies(h):
            copy.start()
    for h in range(heads):
        for copy in copies(h):
            copy.wait()


def final_products(first, heads, scalars, tokens, base, got, before):
    rows, cols = tokens[0].shape
    operands = [*scalars, *tokens, *base, got]
    specs = [SMEM, SMEM] + [VMEM] * 9
    aliases = {}
    if before is not None:
        aliases = {len(operands) + n: n for n in range(4)}
        operands += list(before)
        specs += [ANY] * 4
    return pl.pallas_call(
        functools.partial(final_kernel, first, heads),
        out_shape=[jax.ShapeDtypeStruct((rows, cols), BF16)] * 4,
        in_specs=specs,
        out_specs=[ANY] * 4,
        scratch_shapes=[pltpu.VMEM((rows, heads * DH), BF16)] * 4
        + [
            pltpu.VMEM((rows, DH), F32),
            pltpu.VMEM((rows, DH), F32),
            pltpu.VMEM((heads, 2 * DH, 2 * DH), BF16),
            pltpu.SemaphoreType.DMA((4, heads)),
        ],
        input_output_aliases=aliases,
        compiler_params=pltpu.CompilerParams(vmem_limit_bytes=END_LIMIT),
        cost_estimate=SHORT,
        name="final_products",
    )(*operands)


def exchange_body(queries, key_rows, value_rows, grad_out, packing):
    place = lax.axis_index("seq").astype(jnp.int32).reshape(1)
    scalars = (packing, place)
    tokens = (queries, key_rows, value_rows, grad_out)
    starts = [sum(SIZES[:c]) for c in range(len(SIZES))]
    near = [(i, i ^ 1) for i in range(4)]
    across = [(i, 3 - i) for i in range(4)]

    count = len(SIZES)
    one, two, three = [None] * count, [None] * count, [None] * count
    early = local_sums((message_one,), 0, SIZES[:1], scalars, tokens, packing, FIRST_LIMIT)[0]
    last = early[0]
    inside, out, base = None, None, [None] * count
    for what, c in ORDER:
        if what == "one":
            one[c] = lax.ppermute(early[c], "seq", near)
        elif what == "early":
            early += local_sums(
                (message_one,), SIZES[0], SIZES[1:], scalars, tokens, last, SUMS_LIMIT
            )[0]
            last = early[-1]
        elif what == "own_two":
            (own_two,) = local_sums((message_two,), 0, SIZES, scalars, tokens, last, SUMS_LIMIT)
            last = own_two[0]
        elif what == "own_three":
            (own_three,) = local_sums(
                (message_three,), 0, SIZES, scalars, tokens, last, SUMS_LIMIT
            )
            last = own_three[0]
        elif what == "base":
            got = (one[c], two[c])
            base[c] = base_products(starts[c], SIZES[c], scalars, tokens, inside, got, last)
            last = base[c][0]
        elif what == "two":
            last = join(message_two, scalars, one[c], own_two[c], last)
            two[c] = lax.ppermute(last, "seq", across)
        elif what == "three":
            last = join(message_three, scalars, two[c], own_three[c], last)
            three[c] = lax.ppermute(last, "seq", near)
        elif what == "in":
            first = 0 if inside is None else sum(IN_SIZES[:c])
            inside = inside_products(first, IN_SIZES[c], scalars, tokens, inside, last)
            last = inside[0]
        else:
            out = final_products(starts[c], SIZES[c], scalars, tokens, base[c], three[c], out)
            last = out[0]
    return tuple(out)


highest = lax.Precision.HIGHEST


def carried_in(value, axis, combine, identity, reverse):
    length, index = (lax.axis_size(axis), lax.axis_index(axis))
    everything = jax.tree.map(lambda part: lax.all_gather(part, axis), value)
    start = jax.tree.map(
        lambda part, zero: jnp.broadcast_to(jnp.asarray(zero, part.dtype), part.shape),
        value,
        identity,
    )

    def turn(k, before):
        at = length - 1 - k if reverse else k
        reached = at > index if reverse else at < index
        new = combine(before, jax.tree.map(lambda part: part[at], everything))
        return jax.tree.map(lambda a, b: jnp.where(reached, a, b), new, before)

    return lax.fori_loop(0, length, turn, start)


def block_info(packing, first_block, block_count):
    seg_starts = packing[:, 0]
    seg_ends = packing[:, 1]
    pair_col = packing[:, 2]
    role_col = packing[:, 3]
    blocks = first_block + jnp.arange(block_count, dtype=jnp.int32)
    segment = jnp.sum((seg_starts[None, :] <= blocks[:, None]).astype(jnp.int32), axis=1) - 1
    seg_ranks = jnp.arange(seg_starts.shape[0], dtype=jnp.int32)
    select = segment[:, None] == seg_ranks[None, :]
    block_role = jnp.sum(jnp.where(select, role_col[None, :], 0), axis=1)
    block_pair = jnp.sum(jnp.where(select, pair_col[None, :], 0), axis=1)
    opening = jnp.sum(jnp.where(select, seg_starts[None, :], 0), axis=1)
    prompt_sel = (segment // 3 * 3)[:, None] == seg_ranks[None, :]
    prompt_len = jnp.sum(jnp.where(prompt_sel, (seg_ends - seg_starts)[None, :], 0), axis=1)
    position = (blocks - opening)[:, None] * BLK + jnp.arange(BLK, dtype=jnp.int32)[None, :]
    visible = position + 1 + jnp.where(block_role != 0, prompt_len * BLK, 0)[:, None]
    tok_scale = lax.rsqrt((visible * DH).astype(jnp.float32))
    return (segment, block_role, block_pair, tok_scale)


def link_combine(before, behind):
    back_a, open_a, state_a = before
    back_b, open_b, state_b = behind
    empty_b = open_b < 0.0
    joins = (back_b == open_b) & (open_a == back_b) | empty_b
    state = state_b + jnp.where(joins, state_a, jnp.zeros_like(state_a))
    back_id = jnp.where(open_a < 0.0, back_b, back_a)
    open_id = jnp.where(empty_b, open_a, open_b)
    return (back_id, open_id, state)


def pick_state(carry_open, carry_state, block_ids, allowed):
    chosen = (carry_open == block_ids.astype(jnp.float32)) & allowed
    return jnp.where(chosen[:, None, None, None], carry_state[None], 0.0)


def masked_sum(flags, states):
    return jnp.einsum("j,jhde->hde", flags.astype(jnp.float32), states, precision=highest)


def split_state(state):
    upper = state.astype(jnp.bfloat16)
    upper_wide = lax.optimization_barrier(upper).astype(jnp.float32)
    lower = (state - upper_wide).astype(jnp.bfloat16)
    return (upper, lower)


def state_product(form, token_rows, parts):
    first = jnp.einsum(form, token_rows, parts[0], preferred_element_type=jnp.float32)
    return first + jnp.einsum(form, token_rows, parts[1], preferred_element_type=jnp.float32)


def body(queries, key_rows, value_rows, grad_out, packing):
    block_count = queries.shape[0] // BLK
    local_heads = queries.shape[1] // DH
    group_count = queries.shape[0] // GROUP
    final_index = block_count - 1
    first_block = lax.axis_index("seq") * block_count
    segment, block_role, block_pair, tok_scale = block_info(packing, first_block, block_count)
    dpo_sign = jnp.where(block_role == 2, -1.0, 1.0).astype(jnp.float32)
    q_blocks = queries.reshape(block_count, BLK, local_heads, DH)
    k_blocks = key_rows.reshape(block_count, BLK, local_heads, DH)
    v_blocks = value_rows.reshape(block_count, BLK, local_heads, DH)
    weight = (dpo_sign[:, None] * tok_scale)[:, :, None, None]
    g_blocks = (
        weight * grad_out.reshape(block_count, BLK, local_heads, DH).astype(jnp.float32)
    ).astype(jnp.bfloat16)
    block_kv = jnp.einsum("bshd,bshe->bhde", k_blocks, v_blocks, preferred_element_type=jnp.float32)
    block_qg = jnp.einsum("bshd,bshe->bhde", q_blocks, g_blocks, preferred_element_type=jnp.float32)
    group_of = jnp.arange(block_count, dtype=jnp.int32) // (GROUP // BLK)
    same_seg = segment[:, None] == segment[None, :]
    link = same_seg & (group_of[None, :] < group_of[:, None])
    seg_first = segment[0].astype(jnp.float32)
    seg_last = segment[final_index].astype(jnp.float32)
    neutral = jnp.full((), -1.0, jnp.float32)
    zero_state = jnp.zeros((local_heads, DH, DH), jnp.float32)
    is_prompt = block_role == 0
    is_reply = block_role != 0
    pair_count = packing.shape[0] // 3
    pair_hot = (block_pair[:, None] == jnp.arange(pair_count, dtype=jnp.int32)[None, :]).astype(
        jnp.float32
    )
    fwd_seg = masked_sum(segment == segment[final_index], block_kv)
    carried = carried_in(
        (seg_first, seg_last, fwd_seg), "seq", link_combine, (neutral, neutral, zero_state), False
    )
    prompt_part = jnp.einsum(
        "jp,jhde->phde",
        pair_hot * is_prompt[:, None].astype(jnp.float32),
        block_kv,
        precision=highest,
    )
    prompt_all = lax.psum(prompt_part, "seq")
    outside_in = pick_state(carried[1], carried[2], segment, is_reply | is_prompt)
    outside_in = outside_in + jnp.einsum(
        "bp,phde->bhde",
        pair_hot * is_reply[:, None].astype(jnp.float32),
        prompt_all,
        precision=highest,
    )
    rev_seg = masked_sum(segment == segment[0], block_qg)
    returned = carried_in(
        (seg_last, seg_first, rev_seg), "seq", link_combine, (neutral, neutral, zero_state), True
    )
    reply_part = jnp.einsum(
        "jp,jhde->phde",
        pair_hot * is_reply[:, None].astype(jnp.float32),
        block_qg,
        precision=highest,
    )
    reply_all = lax.psum(reply_part, "seq")
    outside_back = pick_state(returned[1], returned[2], segment, is_reply | is_prompt)
    outside_back = outside_back + jnp.einsum(
        "bp,phde->bhde",
        pair_hot * is_prompt[:, None].astype(jnp.float32),
        reply_all,
        precision=highest,
    )
    link_f = link.astype(jnp.float32)
    state = jnp.einsum("bj,jhde->bhde", link_f, block_kv, precision=highest) + outside_in
    back_state = jnp.einsum("bj,bhde->jhde", link_f, block_qg, precision=highest) + outside_back
    state_parts = split_state(state)
    back_parts = split_state(back_state)
    tok_seg = jnp.repeat(segment, BLK).reshape(group_count, GROUP)
    places = jnp.arange(GROUP, dtype=jnp.int32)
    causal = (tok_seg[:, :, None] == tok_seg[:, None, :]) & (
        places[None, :, None] >= places[None, None, :]
    )
    q_groups = queries.reshape(group_count, GROUP, local_heads, DH)
    k_groups = key_rows.reshape(group_count, GROUP, local_heads, DH)
    v_groups = value_rows.reshape(group_count, GROUP, local_heads, DH)
    g_groups = g_blocks.reshape(group_count, GROUP, local_heads, DH)
    scores = jnp.einsum("cshd,cthd->chst", q_groups, k_groups, preferred_element_type=jnp.float32)
    attn_weights = jnp.where(causal[:, None], scores, 0.0).astype(jnp.bfloat16)
    inside = jnp.einsum(
        "chst,cthd->cshd", attn_weights, v_groups, preferred_element_type=jnp.float32
    )
    inside = inside.reshape(block_count, BLK, local_heads, DH)
    outside = state_product("bshd,bhde->bshe", q_blocks, state_parts)
    attended = (tok_scale[:, :, None, None] * (inside + outside)).astype(jnp.bfloat16)
    back_raw = jnp.einsum("cshd,cthd->chst", g_groups, v_groups, preferred_element_type=jnp.float32)
    back_weights = jnp.where(causal[:, None], back_raw, 0.0).astype(jnp.bfloat16)
    grad_q = jnp.einsum(
        "chst,cthd->cshd", back_weights, k_groups, preferred_element_type=jnp.float32
    )
    grad_q = grad_q.reshape(block_count, BLK, local_heads, DH)
    grad_q = grad_q + state_product("bshe,bhde->bshd", g_blocks, state_parts)
    grad_k = jnp.einsum(
        "chst,cshd->cthd", back_weights, q_groups, preferred_element_type=jnp.float32
    )
    grad_k = grad_k.reshape(block_count, BLK, local_heads, DH)
    grad_k = grad_k + state_product("bshe,bhde->bshd", v_blocks, back_parts)
    grad_v = jnp.einsum(
        "chst,cshd->cthd", attn_weights, g_groups, preferred_element_type=jnp.float32
    )
    grad_v = grad_v.reshape(block_count, BLK, local_heads, DH)
    grad_v = grad_v + state_product("bshd,bhde->bshe", k_blocks, back_parts)
    rows = queries.shape[0]
    columns = queries.shape[1]
    return (
        attended.reshape(rows, columns),
        grad_q.astype(jnp.bfloat16).reshape(rows, columns),
        grad_k.astype(jnp.bfloat16).reshape(rows, columns),
        grad_v.astype(jnp.bfloat16).reshape(rows, columns),
    )


def solution(mesh):
    tokens = P(("grp", "seq"), "head")

    def program(queries, key_rows, value_rows, grad_out, packing):
        rows = queries.shape[0] // mesh.shape["grp"] // mesh.shape["seq"]
        heads = queries.shape[1] // mesh.shape["head"] // DH
        pairs = packing.shape[0] // mesh.shape["grp"] // 3
        four = mesh.shape["seq"] == 4 and pairs == 1
        fits = rows == GROUP and heads == sum(SIZES)
        return jax.shard_map(
            exchange_body if four and fits else body,
            mesh=mesh,
            in_specs=(tokens,) * 4 + (P("grp", None),),
            out_specs=(tokens,) * 4,
            check_vma=False,
        )(queries, key_rows, value_rows, grad_out, packing)

    return program
```
